128 devices in a mesh: dp: 2 (over core), expert: 64 (over z, y, x).
Axes of the slice: x: 4, y: 4, z: 4, core: 2. Of those that a mesh axis runs over, the one named last changes fastest.
Arguments:
- hidden: bfloat16 [32768, 2, 1024], P(('dp', 'expert')), may hold values from -0.75 to 0.75
- grad_out: bfloat16 [32768, 3584], P(('dp', 'expert')), may hold values from -6 to 6
- gates: bfloat16 [32768, 2], P(('dp', 'expert')), may hold values from 0.099609375 to 1
- expert_ids: int32 [32768, 2], P(('dp', 'expert')), may hold values from 0 to 63, all different within a row; in each aligned block of 256 rows (0 to 255, 256 to 511, ...) at most 10 rows name the same one
- weight: bfloat16 [64, 1024, 3584], P('expert', 'dp'), may hold values from -0.09375 to 0.09375
Outputs:
- grad_hidden: bfloat16 [32768, 2, 1024], P(('dp', 'expert'))
- grad_gates: float32 [32768, 2], P(('dp', 'expert'))
- weight_grad: bfloat16 [64, 1024, 3584], P('expert', 'dp')
The draws below stay inside these ranges and needn't reach their ends.
Inputs may be any that keep to these rules, and one draw needn't show every extreme that they name: `expert_ids`: each token names 2 different experts; among the tokens of one device no expert is named more than 10 times, a bound that some block reaches.
All inputs are finite; a program needn't handle non-finite values.
Results may differ from the reference program's by a relative error of at most 0.0059.
Values may be sent and summed in bfloat16 or wider, within the bound.
No kernel may reach another device: no remote copies, remote signals or barrier semaphores. Data moves between devices by JAX's collectives and lax.ppermute only.
A program may use at most 128 MiB of HBM per device.

```python
import math
import jax
import jax.numpy as jnp
import numpy as np
from jax import lax

D = 3584
F = 1024
TOP = 2
TOK_DEV = 256
EXPERTS = 64
CAP = 10
TOKENS = 32768
N_DP = 2
N_EXPERT = 64


def levels(key, dims, pieces, smallest, top_value):
    factor_of, own = 1.0, jax.random.fold_in(key, 6)
    for dim, parts in pieces:
        draws = jnp.exp(jax.random.uniform(jax.random.fold_in(own, dim), (parts,), jnp.float32, smallest / len(pieces), top_value / len(pieces)))
        factor_of = factor_of * jnp.repeat(draws, dims[dim] // parts).reshape([-1 if axis == dim else 1 for axis in range(len(dims))])
    return factor_of


def routed_block(own_key, own, number, rows, number_of, top, bound, skew):
    ranking = jax.random.permutation(own_key, number_of)
    packed, common = shares(number_of, rows * top, bound, skew, True), shares(number_of, rows * top, bound, skew, False)
    places = jnp.arange(number_of)

    def named(sizes, turn):
        used = int((sizes > 0).sum())
        fixed = max(1, used // 4)
        moved = fixed + (places - fixed + turn * (used - fixed)) % max(1, number_of - fixed)
        return jnp.zeros((number_of,), jnp.int32).at[ranking[jnp.where(places < fixed, places, moved)]].set(jnp.asarray(sizes, jnp.int32))

    sizes = jnp.where(number % 4 == 0, named(packed, number // 4), named(common, number - number // 4 - 1))
    mixed = jax.random.permutation(jax.random.fold_in(own, 3), number_of)
    giver, taker = mixed[0:number_of // 2 * 2:2], mixed[1:number_of // 2 * 2:2]
    room = jnp.minimum(sizes[giver] - 1, bound - sizes[taker]) // 2
    room = jnp.where((giver == ranking[0]) | (taker == ranking[0]) | (sizes[taker] == 0), 0, jnp.maximum(room, 0))
    moved = jax.random.randint(jax.random.fold_in(own, 4), (number_of // 2,), 0, 1 << 20) % (room + 1)
    sizes = sizes.at[giver].add(-moved).at[taker].add(moved)
    labels = jnp.searchsorted(jnp.cumsum(sizes), jnp.arange(rows * top), side="right").astype(jnp.int32)
    table = labels.reshape(top, rows).T
    table = table[jax.random.permutation(jax.random.fold_in(own, 1), rows)]
    turn = jax.random.randint(jax.random.fold_in(own, 2), (rows, 1), 0, top)
    return jnp.take_along_axis(table, (jnp.arange(top)[None, :] + turn) % top, axis=1)


def shares(number_of, total, reach, skew, full):
    weights = [(1 << 20) // math.isqrt(rank ** skew) + 1 for rank in range(1, number_of + 1)]
    largest = reach if full else min(reach, max(-(-total // number_of), total * weights[0] // sum(weights)))
    least = 1 if total - largest >= number_of - 1 else 0
    counts, spare = [largest] + [least] * (number_of - 1), total - largest - least * (number_of - 1)
    while spare > 0:
        candidates = [i for i in range(1, number_of) if counts[i] < largest] or [i for i in range(1, number_of) if counts[i] < reach]
        whole, remaining = sum([weights[i] for i in candidates]), spare
        for i in candidates:
            addition = min(reach - counts[i], max(1, remaining * weights[i] // whole), spare)
            counts[i] = counts[i] + addition
            spare = spare - addition
    return np.array(counts)


def centred(rng, extent, scale, reach, shards=(), kind=jnp.bfloat16):
    result = scale * jax.random.normal(rng, extent, jnp.float32)
    if shards:
        result = result * levels(rng, extent, shards, -0.22, 0.18)
    return jnp.clip(result, -reach, reach).astype(kind)


def setup_inputs(seed: int = 0) -> dict:
    arg_keys = jax.random.split(jax.random.key(seed), 6)
    hidden = centred(arg_keys[0], (TOKENS, TOP, F), 0.125, 0.75, ((0, 128),))
    grad_out = centred(arg_keys[1], (TOKENS, D), 1.0, 6.0, ((0, 128),))
    gates = jnp.clip(jnp.exp(math.log(1.0) - 2.306499 * jax.random.uniform(arg_keys[2], (TOKENS, TOP), jnp.float32) ** levels(arg_keys[2], (TOKENS, TOP), ((0, 128),), -0.2, 0.2)), 0.099609375, 1.0).astype(jnp.bfloat16)
    expert_ids_keys = jax.random.split(jax.random.fold_in(arg_keys[3], 1), TOKENS // TOK_DEV)
    expert_ids_turns = jax.random.permutation(jax.random.fold_in(arg_keys[3], 3), TOKENS // TOK_DEV)
    expert_ids = jax.vmap(lambda own, number: routed_block(jax.random.fold_in(arg_keys[3], 2), own, number, TOK_DEV, EXPERTS, TOP, CAP, 2))(expert_ids_keys, expert_ids_turns).reshape((TOKENS, TOP))
    weight = centred(arg_keys[4], (EXPERTS, F, D), D ** -0.5, 0.09375, ((0, 64), (1, 2)))
    return dict(hidden=hidden, grad_out=grad_out, gates=gates, expert_ids=expert_ids, weight=weight)


def reference(hidden, grad_out, gates, expert_ids, weight):
    devices = N_DP * N_EXPERT
    per_device = TOK_DEV * TOP
    slot_count = N_EXPERT * CAP
    routed = expert_ids.reshape(devices, per_device)
    expert_range = jnp.arange(EXPERTS, dtype=jnp.int32)
    onehot = (routed[:, :, None] == expert_range[None, None, :]).astype(jnp.int32)
    rank_in = jnp.sum((jnp.cumsum(onehot, axis=1) - 1) * onehot, axis=2).astype(jnp.int32)
    device_index = jnp.arange(devices, dtype=jnp.int32)[:, None]
    dp_rows = jnp.broadcast_to(device_index // N_EXPERT, (devices, per_device)).astype(jnp.int32)
    source_index = jnp.broadcast_to(device_index % N_EXPERT, (devices, per_device)).astype(jnp.int32)
    slot_index = (source_index * CAP + rank_in).astype(jnp.int32)
    flat_index = jnp.arange(devices * per_device, dtype=jnp.int32).reshape(devices, per_device)
    sentinel = TOKENS * TOP
    table = jnp.full((N_DP, EXPERTS, slot_count), sentinel, jnp.int32)
    table = table.at[dp_rows, routed, slot_index].set(flat_index)
    hidden_rows = jnp.concatenate([hidden.reshape(TOKENS * TOP, F), jnp.zeros((1, F), hidden.dtype)], axis=0)
    grad_rows = jnp.concatenate([grad_out, jnp.zeros((1, D), grad_out.dtype)], axis=0)
    gate_rows = jnp.concatenate([gates.reshape(TOKENS * TOP), jnp.zeros((1,), gates.dtype)], axis=0)

    def per_expert(operands):
        expert_weight, rows_table = operands
        flat_rows = rows_table.reshape(N_DP * slot_count)
        taken_hidden = hidden_rows[flat_rows]
        taken_grad = grad_rows[flat_rows // TOP]
        taken_gate = gate_rows[flat_rows]
        raw_grad = lax.dot_general(taken_grad, expert_weight, (((1,), (1,)), ((), ())),
                                   preferred_element_type=jnp.float32).astype(jnp.bfloat16)
        scaled = (taken_gate.astype(jnp.float32)[:, None] * taken_grad.astype(jnp.float32)).astype(jnp.bfloat16)
        partials = jnp.einsum('isf,isd->ifd',
                              taken_hidden.reshape(N_DP, slot_count, F).astype(jnp.float32),
                              scaled.reshape(N_DP, slot_count, D).astype(jnp.float32))
        rounded = lax.optimization_barrier(partials.astype(jnp.bfloat16))
        summed = jnp.sum(rounded.astype(jnp.float32), axis=0).astype(jnp.bfloat16)
        return raw_grad, summed

    table_by_expert = jnp.transpose(table, (1, 0, 2))
    raw_all, weight_grad = lax.map(per_expert, (weight, table_by_expert))
    raw_flat = jnp.zeros((TOKENS * TOP + 1, F), jnp.bfloat16)
    raw_flat = raw_flat.at[table_by_expert.reshape(-1)].set(raw_all.reshape(-1, F))
    raw_tok = raw_flat[:TOKENS * TOP].reshape(TOKENS, TOP, F).astype(jnp.float32)
    grad_hidden = (gates.astype(jnp.float32)[:, :, None] * raw_tok).astype(jnp.bfloat16)
    grad_gates = jnp.sum(hidden.astype(jnp.float32) * raw_tok, axis=2)
    return grad_hidden, grad_gates, weight_grad
```

```python
import functools

import jax
import jax.numpy as jnp
from jax import lax
from jax.experimental import pallas as pl
from jax.experimental.pallas import tpu as pltpu
from jax.sharding import PartitionSpec as P

T = 256
A = 512
E = 64
D = 3584
F = 1024
COL = 512
FOLD = COL // 4
BLK = COL + FOLD
NG = D // COL
NH = F // COL
MSG = BLK * (NG + NH)
RET = F + F // 4
ROWS = 512
OVER = 128
BF = jnp.bfloat16
F32 = jnp.float32
VMEM = 56 * 1024 * 1024


def iota(shape, axis):
    return lax.broadcasted_iota(jnp.int32, shape, axis)


def dot(a, b):
    return jnp.dot(a, b, preferred_element_type=F32)


def dot_nt(a, b):
    return lax.dot_general(a, b, (((1,), (1,)), ((), ())), preferred_element_type=F32)


def rank_maps(ids):
    experts = iota((E, T), 0)
    o0 = (ids[0:1, :] == experts).astype(F32)
    o1 = (ids[1:2, :] == experts).astype(F32)
    earlier = (iota((T, T), 0) < iota((T, T), 1)).astype(BF)
    count = dot((o0 + o1).astype(BF), earlier)
    return (o0 * (count + 1.0)).astype(BF), (o1 * (count + 1.0)).astype(BF)


def interleave(k):
    return (iota((T, A), 1) == 2 * iota((T, A), 0) + k).astype(BF)


def spread():
    return (jnp.right_shift(iota((ROWS, E), 0), 3) == iota((ROWS, E), 1)).astype(BF)


def pack_kernel(ids_ref, gates_ref, grad_ref, hid_ref, out_ref, sm, sf, hm, hf):
    j = pl.program_id(0)

    @pl.when(j == 0)
    def _():
        r0, r1 = rank_maps(ids_ref[...])
        rows = spread()
        by_token = dot(rows, (r0.astype(F32) + r1.astype(F32)).astype(BF)).astype(jnp.int32)
        row = iota((ROWS, T), 0)
        sm[...] = (by_token == (row & 7) + 1).astype(F32).astype(BF)
        over = by_token == (row & 1) + 9
        quarter = jnp.right_shift(row, 1) & 3
        for q in range(4):
            sf[:, q * T : (q + 1) * T] = (over & (quarter == q)).astype(F32).astype(BF)
        p0, p1 = interleave(0), interleave(1)
        by_assign = dot(rows, (dot(r0, p0) + dot(r1, p1)).astype(BF)).astype(jnp.int32)
        gates = gates_ref[...]
        gate = dot(gates, p0)[0:1, :] + dot(gates, p1)[1:2, :]
        row = iota((ROWS, A), 0)
        hm[...] = jnp.where(by_assign == (row & 7) + 1, gate, 0.0).astype(BF)
        over = by_assign == (row & 1) + 9
        quarter = jnp.right_shift(row, 1) & 3
        for q in range(4):
            hf[:, q * A : (q + 1) * A] = jnp.where(over & (quarter == q), gate, 0.0).astype(BF)

    def emit(main_sel, fold_sel, x):
        out_ref[:, :COL] = dot(main_sel[...], x).astype(BF)
        stacked = jnp.concatenate([x[:, q * FOLD : (q + 1) * FOLD] for q in range(4)], axis=0)
        out_ref[:, COL:] = dot(fold_sel[...], stacked).astype(BF)

    @pl.when(j < NG)
    def _():
        emit(sm, sf, grad_ref[...])

    @pl.when(j >= NG)
    def _():
        emit(hm, hf, hid_ref[...])


def pack(ids, gates, grad, hid):
    return pl.pallas_call(
        pack_kernel,
        grid=(NG + NH,),
        in_specs=[
            pl.BlockSpec((2, T), lambda j: (0, 0)),
            pl.BlockSpec((2, T), lambda j: (0, 0)),
            pl.BlockSpec((T, COL), lambda j: (0, jnp.minimum(j, NG - 1))),
            pl.BlockSpec((A, COL), lambda j: (0, jnp.maximum(j - NG, 0))),
        ],
        out_specs=pl.BlockSpec((ROWS, BLK), lambda j: (0, j)),
        out_shape=jax.ShapeDtypeStruct((ROWS, MSG), BF),
        scratch_shapes=[
            pltpu.VMEM((ROWS, T), BF),
            pltpu.VMEM((ROWS, 4 * T), BF),
            pltpu.VMEM((ROWS, A), BF),
            pltpu.VMEM((ROWS, 4 * A), BF),
        ],
        compiler_params=pltpu.CompilerParams(vmem_limit_bytes=VMEM),
        name="pack",
    )(ids, gates, grad, hid)


def select_kernel(ids_ref, main_ref, fold_ref):
    r0, r1 = rank_maps(ids_ref[...])
    by_assign = dot(spread(), (dot(r0, interleave(0)) + dot(r1, interleave(1))).astype(BF))
    by_assign = by_assign.T.astype(jnp.int32)
    row = iota((A, ROWS), 1)
    main_ref[...] = (by_assign == (row & 7) + 1).astype(F32).astype(BF)
    fold_ref[...] = (by_assign == (row & 1) + 9).astype(F32).astype(BF)


def select(ids):
    shape = jax.ShapeDtypeStruct((A, ROWS), BF)
    return pl.pallas_call(
        select_kernel,
        out_shape=(shape, shape),
        compiler_params=pltpu.CompilerParams(vmem_limit_bytes=VMEM),
        name="select",
    )(ids)


def unfold_matrix():
    i, j = iota((ROWS, ROWS), 0), iota((ROWS, ROWS), 1)
    home = jnp.right_shift(i & 127, 1) * 8 + jnp.right_shift(i, 7) * 2 + (i & 1)
    return (home == j).astype(F32).astype(BF)


def fold_matrix():
    j, i = iota((ROWS, ROWS), 0), iota((ROWS, ROWS), 1)
    home = jnp.right_shift(i & 127, 1) * 8 + jnp.right_shift(i, 7) * 2 + (i & 1)
    return (home == j).astype(F32).astype(BF)


def unfold(matrix, folded):
    rows = dot(matrix, folded).astype(BF)
    return jnp.concatenate([rows[q * OVER : (q + 1) * OVER, :] for q in range(4)], axis=1)


def raw_kernel(msg_ref, w_ref, out_ref, acc, um):
    j = pl.program_id(0)

    @pl.when(j == 0)
    def _():
        um[...] = unfold_matrix()
        acc[...] = jnp.zeros_like(acc)

    w = w_ref[...]
    acc[:ROWS, :] += dot_nt(msg_ref[:, :COL], w)
    acc[ROWS:, :] += dot_nt(unfold(um[...], msg_ref[:, COL:]), w)

    @pl.when(j == NG - 1)
    def _():
        out_ref[:, :F] = acc[:ROWS, :].astype(BF)
        over = acc[ROWS:, :].astype(BF)
        stacked = jnp.concatenate([over[:, q * 256 : (q + 1) * 256] for q in range(4)], axis=0)
        out_ref[:, F:] = dot(fold_matrix(), stacked).astype(BF)


def raw_rows(msg, weight):
    return pl.pallas_call(
        raw_kernel,
        grid=(NG,),
        in_specs=[
            pl.BlockSpec((ROWS, BLK), lambda j: (0, j)),
            pl.BlockSpec((F, COL), lambda j: (0, j)),
        ],
        out_specs=pl.BlockSpec((ROWS, RET), lambda j: (0, 0)),
        out_shape=jax.ShapeDtypeStruct((ROWS, RET), BF),
        scratch_shapes=[pltpu.VMEM((ROWS + OVER, F), F32), pltpu.VMEM((ROWS, ROWS), BF)],
        compiler_params=pltpu.CompilerParams(vmem_limit_bytes=VMEM),
        name="raw",
    )(msg, weight)


def partial_kernel(add, half_ref, msg_ref, hid_ref, *rest):
    if add:
        got_ref, out_ref, ht, um = rest
    else:
        out_ref, ht, um = rest
    j = pl.program_id(0)

    @pl.when(j == 0)
    def _():
        um[...] = unfold_matrix()
        ht[:, :ROWS] = hid_ref[:, :COL].T
        ht[:, ROWS:] = unfold(um[...], hid_ref[:, COL:]).T

    value = dot(ht[:, :ROWS], msg_ref[:, :COL])
    value += dot(ht[:, ROWS:], unfold(um[...], msg_ref[:, COL:]))
    if add:
        value = value.astype(BF).astype(F32) + got_ref[...].astype(F32)
    out_ref[...] = value.astype(BF)


def partial_half(half, msg, got=None):
    in_specs = [
        pl.BlockSpec((ROWS, BLK), lambda j, half: (0, j)),
        pl.BlockSpec((ROWS, BLK), lambda j, half: (0, NG + half[0])),
    ]
    args = [half, msg, msg]
    block = pl.BlockSpec((COL, COL), lambda j, half: (0, j))
    if got is not None:
        in_specs.append(block)
        args.append(got)
    return pl.pallas_call(
        functools.partial(partial_kernel, got is not None),
        grid_spec=pltpu.PrefetchScalarGridSpec(
            num_scalar_prefetch=1,
            grid=(NG,),
            in_specs=in_specs,
            out_specs=block,
            scratch_shapes=[
                pltpu.VMEM((COL, ROWS + OVER), BF),
                pltpu.VMEM((ROWS, ROWS), BF),
            ],
        ),
        out_shape=jax.ShapeDtypeStruct((COL, D), BF),
        compiler_params=pltpu.CompilerParams(vmem_limit_bytes=VMEM),
        name="partial_own" if got is not None else "partial_other",
    )(*args)


def combine_kernel(main_ref, fold_ref, ret_ref, gate_ref, hid_ref, out_ref, gg_ref):
    folded = ret_ref[:, F:]
    pick = fold_ref[...]
    quarter = jnp.right_shift(iota((1, ROWS), 1), 1) & 3
    gate = gate_ref[...].astype(F32)
    total = jnp.zeros((A, 1), F32)
    for q in range(4):
        cols = slice(q * 256, (q + 1) * 256)
        raw = dot(main_ref[...], ret_ref[:, cols])
        raw += dot(pick * (quarter == q).astype(F32).astype(BF), folded)
        out_ref[:, cols] = (gate * raw).astype(BF)
        total += jnp.sum(hid_ref[:, cols].astype(F32) * raw, axis=1, keepdims=True)
    gg_ref[...] = total


def combine(main_sel, fold_sel, ret, gate, hid):
    return pl.pallas_call(
        combine_kernel,
        out_shape=(jax.ShapeDtypeStruct((A, F), BF), jax.ShapeDtypeStruct((A, 1), F32)),
        compiler_params=pltpu.CompilerParams(vmem_limit_bytes=VMEM),
        name="combine",
    )(main_sel, fold_sel, ret, gate, hid)


def exchange(x):
    width = x.shape[1]
    swapped = lax.all_to_all(
        x.reshape(E, 8, width), "expert", split_axis=0, concat_axis=0, tiled=True
    )
    return swapped.reshape(ROWS, width)


def per_device(hidden, grad_out, gates, expert_ids, weight):
    dp = lax.axis_index("dp").astype(jnp.int32)
    ids = expert_ids.T
    hid = hidden.reshape(A, F)
    msg = exchange(pack(ids, gates.T, grad_out, hid))
    full_weight = lax.all_gather(weight[0], "dp", axis=0, tiled=True)
    main_sel, fold_sel = select(ids)
    ret = exchange(raw_rows(msg, full_weight))
    sent = partial_half((1 - dp).reshape(1), msg)
    got = lax.ppermute(sent, "dp", [(0, 1), (1, 0)])
    weight_grad = partial_half(dp.reshape(1), msg, got)
    grad_hidden, grad_gates = combine(main_sel, fold_sel, ret, gates.reshape(A, 1), hid)
    return grad_hidden.reshape(T, 2, F), grad_gates.reshape(T, 2), weight_grad[None]


def solution(mesh):
    in_specs = (
        P(("dp", "expert"), None, None),
        P(("dp", "expert"), None),
        P(("dp", "expert"), None),
        P(("dp", "expert"), None),
        P("expert", "dp", None),
    )
    out_specs = (
        P(("dp", "expert"), None, None),
        P(("dp", "expert"), None),
        P("expert", "dp", None),
    )
    return jax.shard_map(
        per_device, mesh=mesh, in_specs=in_specs, out_specs=out_specs, check_vma=False
    )
```

```python
import jax
import jax.numpy as jnp
from jax import lax
from jax.experimental import pallas as pl
from jax.experimental.pallas import tpu as pltpu
from jax.sharding import PartitionSpec as P

T = 256
A = 512
E = 64
D = 3584
F = 1024
COL = 512
FOLD = COL // 4
BLK = COL + FOLD
NG = D // COL
NH = F // COL
MSG = BLK * (NG + NH)
RET = F + F // 4
ROWS = 512
OVER = 128
HALF = 256
BF = jnp.bfloat16
F32 = jnp.float32
PARAMS = pltpu.CompilerParams(vmem_limit_bytes=56 * 1024 * 1024)
ANY = pl.BlockSpec(memory_space=pl.ANY)
IN_VMEM = pl.BlockSpec(memory_space=pltpu.VMEM)
IN_SMEM = pl.BlockSpec(memory_space=pltpu.SMEM)


def iota(shape, axis):
    return lax.broadcasted_iota(jnp.int32, shape, axis)


def dot(a, b):
    return jnp.dot(a, b, preferred_element_type=F32)


def dot_nt(a, b):
    return lax.dot_general(a, b, (((1,), (1,)), ((), ())), preferred_element_type=F32)


def columns(j, width=COL):
    return slice(j * width, (j + 1) * width)


def main_cols(j):
    return slice(j * BLK, j * BLK + COL)


def fold_cols(j):
    return slice(j * BLK + COL, (j + 1) * BLK)


def fold_home(i):
    return jnp.right_shift(i & 63, 1) * 8 + jnp.right_shift(i, 6) * 2 + (i & 1)


def unfold_matrix():
    i, j = iota((HALF, HALF), 0), iota((HALF, HALF), 1)
    return (fold_home(i) == j).astype(F32).astype(BF)


def fold_matrix():
    j, i = iota((HALF, HALF), 0), iota((HALF, HALF), 1)
    return (fold_home(i) == j).astype(F32).astype(BF)


def unfold(matrix, folded):
    out = []
    for b in range(2):
        rows = dot(matrix, folded[columns(b, HALF), :]).astype(BF)
        out.append(jnp.concatenate([rows[columns(q, 64), :] for q in range(4)], axis=1))
    return jnp.concatenate(out, axis=0)


def fold(matrix, over):
    out = []
    width = over.shape[1] // 4
    for b in range(2):
        part = over[columns(b, 64), :]
        stacked = jnp.concatenate([part[:, columns(q, width)] for q in range(4)], axis=0)
        out.append(dot(matrix, stacked).astype(BF))
    return jnp.concatenate(out, axis=0)


def rank_maps(ids):
    experts = iota((E, T), 0)
    o0 = (ids[0:1, :] == experts).astype(F32)
    o1 = (ids[1:2, :] == experts).astype(F32)
    earlier = (iota((T, T), 0) < iota((T, T), 1)).astype(F32).astype(BF)
    count = dot((o0 + o1).astype(BF), earlier)
    return o0 * (count + 1.0), o1 * (count + 1.0)


def slots():
    i = iota((ROWS + OVER, 1), 0)
    main = i < ROWS
    expert = jnp.where(main, jnp.right_shift(i, 3), jnp.right_shift(i - ROWS, 1))
    rank = jnp.where(main, (i & 7) + 1, (i & 1) + 9)
    rows = (expert == iota((ROWS + OVER, E), 1)).astype(F32).astype(BF)
    return rows, rank.astype(F32)


def interleave(k):
    return (iota((T, A), 1) == 2 * iota((T, A), 0) + k).astype(F32).astype(BF)


def assignments(r0, r1):
    by_assign = dot(r0.astype(BF), interleave(0)) + dot(r1.astype(BF), interleave(1))
    return by_assign.astype(BF)


def pack_kernel(ids_ref, gates_ref, grad_ref, hid_ref, out_ref, grad, hid, out, sem, osem):
    copies = []
    for j in range(NG):
        copy = pltpu.make_async_copy(
            grad_ref.at[:, columns(j)], grad.at[:, columns(j)], sem.at[j]
        )
        copy.start()
        copies.append(copy)
    hid_copy = pltpu.make_async_copy(hid_ref, hid, sem.at[NG])
    hid_copy.start()
    r0, r1 = rank_maps(ids_ref[...])
    rows, rank = slots()
    sel = (dot(rows, (r0 + r1).astype(BF)) == rank).astype(F32).astype(BF)
    matrix = fold_matrix()
    outs = []

    def emit(j, chosen, x):
        value = dot(chosen, x)
        out[:, main_cols(j)] = value[:ROWS].astype(BF)
        out[:, fold_cols(j)] = fold(matrix, value[ROWS:].astype(BF))
        cols = columns(j, BLK)
        copy = pltpu.make_async_copy(out.at[:, cols], out_ref.at[:, cols], osem.at[j])
        copy.start()
        outs.append(copy)

    for j in range(NG):
        copies[j].wait()
        emit(j, sel, grad[:, columns(j)])
    gates = gates_ref[...]
    gate = dot(gates, interleave(0))[0:1, :] + dot(gates, interleave(1))[1:2, :]
    gated = jnp.where(dot(rows, assignments(r0, r1)) == rank, gate, 0.0).astype(BF)
    hid_copy.wait()
    for j in range(NH):
        emit(NG + j, gated, hid[:, :, columns(j)].reshape(A, COL))
    for copy in outs:
        copy.wait()


def pack(ids, gates, grad, hid):
    return pl.pallas_call(
        pack_kernel,
        in_specs=[IN_VMEM, IN_VMEM, ANY, ANY],
        out_specs=ANY,
        out_shape=jax.ShapeDtypeStruct((ROWS, MSG), BF),
        scratch_shapes=[
            pltpu.VMEM((T, D), BF),
            pltpu.VMEM((T, 2, F), BF),
            pltpu.VMEM((ROWS, MSG), BF),
            pltpu.SemaphoreType.DMA((NG + 1,)),
            pltpu.SemaphoreType.DMA((NG + NH,)),
        ],
        compiler_params=PARAMS,
        name="pack",
    )(ids, gates, grad, hid)


def raw_kernel(dp_ref, msg_ref, own_ref, other_ref, out_ref, msg, w, acc, sem):
    own = pl.ds(pl.multiple_of(dp_ref[0] * COL, COL), COL)
    other = pl.ds(pl.multiple_of((1 - dp_ref[0]) * COL, COL), COL)
    copies = []
    for j in range(NG):
        block, cols = columns(j, BLK), columns(j)
        group = [
            pltpu.make_async_copy(msg_ref.at[:, block], msg.at[:, block], sem.at[j, 0]),
            pltpu.make_async_copy(own_ref.at[:, cols], w.at[own, cols], sem.at[j, 1]),
            pltpu.make_async_copy(other_ref.at[:, cols], w.at[other, cols], sem.at[j, 2]),
        ]
        for copy in group:
            copy.start()
        copies.append(group)
    matrix = unfold_matrix()
    for j in range(NG):
        for copy in copies[j]:
            copy.wait()
        over = unfold(matrix, msg[:, fold_cols(j)])
        rows = jnp.concatenate([msg[:, main_cols(j)], over], axis=0)
        value = dot_nt(rows, w[:, columns(j)])
        if j == 0:
            acc[...] = value
        else:
            acc[...] += value
    out_ref[:, :F] = acc[:ROWS, :].astype(BF)
    out_ref[:, F:] = fold(fold_matrix(), acc[ROWS:, :].astype(BF))


def raw_rows(dp, msg, own, other):
    return pl.pallas_call(
        raw_kernel,
        in_specs=[IN_SMEM, ANY, ANY, ANY],
        out_shape=jax.ShapeDtypeStruct((ROWS, RET), BF),
        scratch_shapes=[
            pltpu.VMEM((ROWS, NG * BLK), BF),
            pltpu.VMEM((F, D), BF),
            pltpu.VMEM((ROWS + OVER, F), F32),
            pltpu.SemaphoreType.DMA((NG, 3)),
        ],
        compiler_params=PARAMS,
        name="raw",
    )(dp, msg, own, other)


def grad_kernel(dp_ref, own_ref, got_ref, out_ref, msgs, hids, ht, out, sem, osem):
    sources = (own_ref, got_ref)
    half = pl.ds(pl.multiple_of((NG + dp_ref[0]) * BLK, FOLD), BLK)
    hid_copies = []
    for i, ref in enumerate(sources):
        copy = pltpu.make_async_copy(ref.at[:, half], hids.at[i], sem.at[NG, i])
        copy.start()
        hid_copies.append(copy)
    copies = []
    for j in range(NG):
        block = columns(j, BLK)
        group = []
        for i, ref in enumerate(sources):
            copy = pltpu.make_async_copy(ref.at[:, block], msgs.at[i, :, block], sem.at[j, i])
            copy.start()
            group.append(copy)
        copies.append(group)
    matrix = unfold_matrix()
    for i in range(2):
        hid_copies[i].wait()
        at = i * (ROWS + OVER)
        ht[:, at : at + ROWS] = hids[i, :, :COL].T
        ht[:, at + ROWS : at + ROWS + OVER] = unfold(matrix, hids[i, :, COL:]).T
    outs = []
    for j in range(NG):
        for copy in copies[j]:
            copy.wait()
        rows = []
        for i in range(2):
            rows.append(msgs[i, :, main_cols(j)])
            rows.append(unfold(matrix, msgs[i, :, fold_cols(j)]))
        cols = columns(j)
        out[:, cols] = dot(ht[...], jnp.concatenate(rows, axis=0)).astype(BF)
        copy = pltpu.make_async_copy(out.at[:, cols], out_ref.at[:, cols], osem.at[j])
        copy.start()
        outs.append(copy)
    for copy in outs:
        copy.wait()


def weight_rows(dp, own, got):
    return pl.pallas_call(
        grad_kernel,
        in_specs=[IN_SMEM, ANY, ANY],
        out_specs=ANY,
        out_shape=jax.ShapeDtypeStruct((COL, D), BF),
        scratch_shapes=[
            pltpu.VMEM((2, ROWS, NG * BLK), BF),
            pltpu.VMEM((2, ROWS, BLK), BF),
            pltpu.VMEM((COL, 2 * (ROWS + OVER)), BF),
            pltpu.VMEM((COL, D), BF),
            pltpu.SemaphoreType.DMA((NG + 1, 2)),
            pltpu.SemaphoreType.DMA((NG,)),
        ],
        compiler_params=PARAMS,
        name="weight_grad",
    )(dp, own, got)


def select_kernel(ids_ref, out_ref):
    r0, r1 = rank_maps(ids_ref[...])
    rows, rank = slots()
    chosen = (dot(rows, assignments(r0, r1)) == rank).astype(F32)
    out_ref[...] = chosen.T.astype(BF)


def select(ids):
    return pl.pallas_call(
        select_kernel,
        out_shape=jax.ShapeDtypeStruct((A, ROWS + OVER), BF),
        compiler_params=PARAMS,
        name="select",
    )(ids)


def combine_kernel(sel_ref, ret_ref, gates_ref, hid_ref, out_ref, gg_ref, part):
    over = unfold(unfold_matrix(), ret_ref[:, F:])
    raw = dot(sel_ref[...], jnp.concatenate([ret_ref[:, :F], over], axis=0))
    gates = gates_ref[...].astype(F32)
    row, token = iota((A, T), 0), iota((A, T), 1)
    spread = jnp.where(row == 2 * token, gates[0:1, :], 0.0)
    spread += jnp.where(row == 2 * token + 1, gates[1:2, :], 0.0)
    gate = jnp.sum(spread, axis=1, keepdims=True)
    out_ref[...] = (gate * raw).astype(BF).reshape(T, 2, F)
    product = hid_ref[...].reshape(A, F).astype(F32) * raw
    total = product[:, columns(0, 128)]
    for c in range(1, F // 128):
        total += product[:, columns(c, 128)]
    part[...] = total
    for k in range(2):
        rows = part[pl.ds(k, T, stride=2), :]
        gg_ref[k : k + 1, :] = jnp.sum(rows.T, axis=0, keepdims=True)


def combine(sel, ret, gates, hid):
    return pl.pallas_call(
        combine_kernel,
        out_shape=(jax.ShapeDtypeStruct((T, 2, F), BF), jax.ShapeDtypeStruct((2, T), F32)),
        scratch_shapes=[pltpu.VMEM((A, 128), F32)],
        compiler_params=PARAMS,
        name="combine",
    )(sel, ret, gates, hid)


def exchange(x):
    width = x.shape[1]
    swapped = lax.all_to_all(
        x.reshape(E, 8, width), "expert", split_axis=0, concat_axis=0, tiled=True
    )
    return swapped.reshape(ROWS, width)


def swap(x):
    return lax.ppermute(x, "dp", [(0, 1), (1, 0)])


def per_device(hidden, grad_out, gates, expert_ids, weight):
    dp = lax.axis_index("dp").astype(jnp.int32).reshape(1)
    ids = expert_ids.T
    own = weight[0]
    packed = pack(ids, gates.T, grad_out, hidden)
    other = swap(own)
    packed, other, dp = lax.optimization_barrier((packed, other, dp))
    msg = exchange(packed)
    raw = raw_rows(dp, msg, own, other)
    got = swap(msg)
    ids, msg, raw = lax.optimization_barrier((ids, msg, raw))
    ret = exchange(raw)
    sel = select(ids)
    weight_grad = weight_rows(dp, msg, got)
    ret, weight_grad = lax.optimization_barrier((ret, weight_grad))
    ret = pltpu.with_memory_space_constraint(ret, pltpu.VMEM)
    grad_hidden, grad_gates = combine(sel, ret, gates.T, hidden)
    return grad_hidden, grad_gates.T, weight_grad[None]


def solution(mesh):
    in_specs = (
        P(("dp", "expert"), None, None),
        P(("dp", "expert"), None),
        P(("dp", "expert"), None),
        P(("dp", "expert"), None),
        P("expert", "dp", None),
    )
    out_specs = (
        P(("dp", "expert"), None, None),
        P(("dp", "expert"), None),
        P("expert", "dp", None),
    )
    return jax.shard_map(
        per_device, mesh=mesh, in_specs=in_specs, out_specs=out_specs, check_vma=False
    )
```

```python
import jax
import jax.numpy as jnp
from jax import lax
from jax.experimental import pallas as pl
from jax.experimental.pallas import tpu as pltpu
from jax.sharding import PartitionSpec as P

T = 256
A = 512
E = 64
D = 3584
F = 1024
COL = 512
FOLD = COL // 4
BLK = COL + FOLD
NG = D // COL
NH = F // COL
MSG = BLK * (NG + NH)
RET = F + F // 4
ROWS = 512
OVER = 128
BF = jnp.bfloat16
F32 = jnp.float32
PARAMS = pltpu.CompilerParams(vmem_limit_bytes=36 * 1024 * 1024)
IN_HBM = pl.BlockSpec(memory_space=pltpu.HBM)
IN_VMEM = pl.BlockSpec(memory_space=pltpu.VMEM)
IN_SMEM = pl.BlockSpec(memory_space=pltpu.SMEM)


def keep(x):
    return pltpu.with_memory_space_constraint(x, pltpu.VMEM)


def iota(shape, axis):
    return lax.broadcasted_iota(jnp.int32, shape, axis)


def dot(a, b):
    return jnp.dot(a, b, preferred_element_type=F32)


def dot_nt(a, b):
    return lax.dot_general(a, b, (((1,), (1,)), ((), ())), preferred_element_type=F32)


def columns(j, width=COL):
    return slice(j * width, (j + 1) * width)


def main_cols(j):
    return slice(j * BLK, j * BLK + COL)


def fold_cols(j):
    return slice(j * BLK + COL, (j + 1) * BLK)


def trade(x):
    row = iota((1, 8, 128), 1)
    low, even = row < 4, (row & 2) == 0

    def mix(p, q, shift, first):
        return (
            jnp.where(first, p, pltpu.roll(q, shift, 1)),
            jnp.where(first, pltpu.roll(p, 8 - shift, 1), q),
        )

    b0, b2 = mix(x[0], x[2], 4, low)
    b1, b3 = mix(x[1], x[3], 4, low)
    return mix(b0, b1, 2, even) + mix(b2, b3, 2, even)


def fold(over):
    width = over.shape[1] // 4
    out = []
    for c in range(width // 128):
        parts = []
        for q in range(4):
            at = q * width + c * 128
            parts.append(over[:, at : at + 128].reshape(16, 8, 128))
        out.append(jnp.stack(trade(parts), axis=1).reshape(ROWS, 128).astype(BF))
    return jnp.concatenate(out, axis=1)


def unfold(folded):
    quarters = [[], [], [], []]
    for c in range(folded.shape[1] // 128):
        part = folded[:, columns(c, 128)].astype(F32).reshape(16, 4, 8, 128)
        for q, rows in enumerate(trade([part[:, i] for i in range(4)])):
            quarters[q].append(rows.reshape(OVER, 128).astype(BF))
    return jnp.concatenate([rows for quarter in quarters for rows in quarter], axis=1)


def rank_maps(ids):
    experts = iota((E, T), 0)
    o0 = (ids[0:1, :] == experts).astype(F32)
    o1 = (ids[1:2, :] == experts).astype(F32)
    earlier = (iota((T, T), 0) < iota((T, T), 1)).astype(F32).astype(BF)
    count = dot((o0 + o1).astype(BF), earlier)
    return o0 * (count + 1.0), o1 * (count + 1.0)


def slots():
    i = iota((ROWS + OVER, 1), 0)
    main = i < ROWS
    expert = jnp.where(main, jnp.right_shift(i, 3), jnp.right_shift(i - ROWS, 1))
    rank = jnp.where(main, (i & 7) + 1, (i & 1) + 9)
    rows = (expert == iota((ROWS + OVER, E), 1)).astype(F32).astype(BF)
    return rows, rank.astype(F32)


def interleave(k):
    return (iota((T, A), 1) == 2 * iota((T, A), 0) + k).astype(F32).astype(BF)


def assignments(r0, r1):
    by_assign = dot(r0.astype(BF), interleave(0)) + dot(r1.astype(BF), interleave(1))
    return by_assign.astype(BF)


def pack_kernel(ids_hbm, gates_hbm, grad_hbm, hid_hbm, out_ref, ids, gates, grad, hid, sem):
    first = slice(0, 3 * COL)
    rest = slice(3 * COL, D)
    copies = [
        pltpu.make_async_copy(ids_hbm, ids, sem.at[0]),
        pltpu.make_async_copy(gates_hbm, gates, sem.at[1]),
        pltpu.make_async_copy(grad_hbm.at[:, first], grad.at[:, first], sem.at[2]),
        pltpu.make_async_copy(grad_hbm.at[:, rest], grad.at[:, rest], sem.at[3]),
        pltpu.make_async_copy(hid_hbm, hid, sem.at[4]),
    ]
    for copy in copies:
        copy.start()
    rows, rank = slots()
    copies[0].wait()
    copies[1].wait()
    r0, r1 = rank_maps(ids[...])
    sel = (dot(rows, (r0 + r1).astype(BF)) == rank).astype(F32).astype(BF)
    gate = dot(gates[...], interleave(0))[0:1, :] + dot(gates[...], interleave(1))[1:2, :]
    gated = jnp.where(dot(rows, assignments(r0, r1)) == rank, gate, 0.0).astype(BF)

    def emit(j, chosen, x):
        value = dot(chosen, x)
        out_ref[:, main_cols(j)] = value[:ROWS].astype(BF)
        out_ref[:, fold_cols(j)] = fold(value[ROWS:])

    copies[2].wait()
    for j in range(3):
        emit(j, sel, grad[:, columns(j)])
    copies[3].wait()
    for j in range(3, NG):
        emit(j, sel, grad[:, columns(j)])
    copies[4].wait()
    for j in range(NH):
        emit(NG + j, gated, hid[:, :, columns(j)].reshape(A, COL))


def pack(ids, gates, grad, hid):
    return pl.pallas_call(
        pack_kernel,
        in_specs=[IN_HBM, IN_HBM, IN_HBM, IN_HBM],
        out_specs=IN_VMEM,
        out_shape=pltpu.VMEM((ROWS, MSG), BF),
        scratch_shapes=[
            pltpu.VMEM((2, T), jnp.int32),
            pltpu.VMEM((2, T), BF),
            pltpu.VMEM((T, D), BF),
            pltpu.VMEM((T, 2, F), BF),
            pltpu.SemaphoreType.DMA((5,)),
        ],
        compiler_params=pltpu.CompilerParams(vmem_limit_bytes=50 * 1024 * 1024),
        name="pack",
    )(ids, gates, grad, hid)


def raw_kernel(
    dp_ref, msg_ref, own_ref, other_hbm, out_hbm, keep_hbm, other, over, acc, out, last, sem
):
    weight_copy = pltpu.make_async_copy(other_hbm, other, sem.at[4])
    weight_copy.start()
    outs = [pltpu.make_async_copy(msg_ref, keep_hbm, sem.at[3])]
    outs[0].start()
    for i, weight in enumerate((own_ref, other)):
        value = None
        if i == 1:
            weight_copy.wait()
        for j in range(NG):
            if i == 0:
                over[:, columns(j)] = unfold(msg_ref[:, fold_cols(j)])
            rows = jnp.concatenate([msg_ref[:, main_cols(j)], over[:, columns(j)]], axis=0)
            part = dot_nt(rows, weight[:, columns(j)])
            value = part if value is None else value + part
        half = dp_ref[0] if i == 0 else 1 - dp_ref[0]
        cols = pl.ds(pl.multiple_of(half * COL, COL), COL)
        out[i] = value[:ROWS].astype(BF)
        acc[:, cols] = value[ROWS:]
        copy = pltpu.make_async_copy(out.at[i], out_hbm.at[:, cols], sem.at[i])
        copy.start()
        outs.append(copy)
    last[...] = fold(acc[...])
    copy = pltpu.make_async_copy(last, out_hbm.at[:, F:], sem.at[2])
    copy.start()
    for copy in outs + [copy]:
        copy.wait()


def raw_rows(dp, msg, own, other):
    return pl.pallas_call(
        raw_kernel,
        in_specs=[IN_SMEM, IN_VMEM, IN_VMEM, IN_HBM],
        out_specs=(IN_HBM, IN_HBM),
        out_shape=(
            jax.ShapeDtypeStruct((ROWS, RET), BF),
            jax.ShapeDtypeStruct((ROWS, MSG), BF),
        ),
        scratch_shapes=[
            pltpu.VMEM((COL, D), BF),
            pltpu.VMEM((OVER, D), BF),
            pltpu.VMEM((OVER, F), F32),
            pltpu.VMEM((2, ROWS, COL), BF),
            pltpu.VMEM((ROWS, F // 4), BF),
            pltpu.SemaphoreType.DMA((5,)),
        ],
        compiler_params=pltpu.CompilerParams(vmem_limit_bytes=32 * 1024 * 1024),
        name="raw",
    )(dp, keep(msg), keep(own), other)


def grad_kernel(dp_ref, own_ref, got_ref, out_ref, msgs, hids, ht, out, sem, osem):
    sources = (own_ref, got_ref)
    half = pl.ds(pl.multiple_of((NG + dp_ref[0]) * BLK, FOLD), BLK)
    hid_copies = []
    for i, ref in enumerate(sources):
        copy = pltpu.make_async_copy(ref.at[:, half], hids.at[i], sem.at[NG, i])
        copy.start()
        hid_copies.append(copy)
    copies = []
    for j in range(NG):
        block = columns(j, BLK)
        group = []
        for i, ref in enumerate(sources):
            copy = pltpu.make_async_copy(ref.at[:, block], msgs.at[i, :, block], sem.at[j, i])
            copy.start()
            group.append(copy)
        copies.append(group)
    for i in range(2):
        hid_copies[i].wait()
        at = i * (ROWS + OVER)
        ht[:, at : at + ROWS] = hids[i, :, :COL].T
        ht[:, at + ROWS : at + ROWS + OVER] = unfold(hids[i, :, COL:]).T
    outs = []
    for j in range(NG):
        for copy in copies[j]:
            copy.wait()
        rows = []
        for i in range(2):
            rows.append(msgs[i, :, main_cols(j)])
            rows.append(unfold(msgs[i, :, fold_cols(j)]))
        cols = columns(j)
        out[:, cols] = dot(ht[...], jnp.concatenate(rows, axis=0)).astype(BF)
        copy = pltpu.make_async_copy(out.at[:, cols], out_ref.at[:, cols], osem.at[j])
        copy.start()
        outs.append(copy)
    for copy in outs:
        copy.wait()


def weight_rows(dp, own, got):
    return pl.pallas_call(
        grad_kernel,
        in_specs=[IN_SMEM, IN_HBM, IN_HBM],
        out_specs=IN_HBM,
        out_shape=jax.ShapeDtypeStruct((COL, D), BF),
        scratch_shapes=[
            pltpu.VMEM((2, ROWS, NG * BLK), BF),
            pltpu.VMEM((2, ROWS, BLK), BF),
            pltpu.VMEM((COL, 2 * (ROWS + OVER)), BF),
            pltpu.VMEM((COL, D), BF),
            pltpu.SemaphoreType.DMA((NG + 1, 2)),
            pltpu.SemaphoreType.DMA((NG,)),
        ],
        compiler_params=PARAMS,
        name="weight_grad",
    )(dp, own, got)


def select_kernel(ids_ref, out_ref):
    r0, r1 = rank_maps(ids_ref[...])
    rows, rank = slots()
    chosen = (dot(rows, assignments(r0, r1)) == rank).astype(F32)
    out_ref[...] = chosen.T.astype(BF)


def select(ids):
    return pl.pallas_call(
        select_kernel,
        out_shape=jax.ShapeDtypeStruct((A, ROWS + OVER), BF),
        compiler_params=PARAMS,
        name="select",
    )(ids)


def combine_kernel(sel_ref, ret_ref, gates_ref, hid_ref, out_ref, gg_ref, part):
    over = unfold(ret_ref[:, F:])
    raw = dot(sel_ref[...], jnp.concatenate([ret_ref[:, :F], over], axis=0))
    gates = gates_ref[...].astype(F32)
    row, token = iota((A, T), 0), iota((A, T), 1)
    spread = jnp.where(row == 2 * token, gates[0:1, :], 0.0)
    spread += jnp.where(row == 2 * token + 1, gates[1:2, :], 0.0)
    gate = jnp.sum(spread, axis=1, keepdims=True)
    out_ref[...] = (gate * raw).astype(BF).reshape(T, 2, F)
    product = hid_ref[...].reshape(A, F).astype(F32) * raw
    total = product[:, columns(0, 128)]
    for c in range(1, F // 128):
        total += product[:, columns(c, 128)]
    part[...] = total
    for k in range(2):
        rows = part[pl.ds(k, T, stride=2), :]
        gg_ref[k : k + 1, :] = jnp.sum(rows.T, axis=0, keepdims=True)


def combine(sel, ret, gates, hid):
    return pl.pallas_call(
        combine_kernel,
        out_shape=(jax.ShapeDtypeStruct((T, 2, F), BF), jax.ShapeDtypeStruct((2, T), F32)),
        scratch_shapes=[pltpu.VMEM((A, 128), F32)],
        compiler_params=PARAMS,
        name="combine",
    )(sel, ret, gates, hid)


def exchange(x):
    width = x.shape[1]
    swapped = lax.all_to_all(
        x.reshape(E, 8, width), "expert", split_axis=0, concat_axis=0, tiled=True
    )
    return swapped.reshape(ROWS, width)


def swap(x):
    return lax.ppermute(x, "dp", [(0, 1), (1, 0)])


def per_device(hidden, grad_out, gates, expert_ids, weight):
    dp = lax.axis_index("dp").astype(jnp.int32).reshape(1)
    ids = expert_ids.T
    own = weight[0]
    packed = pack(ids, gates.T, grad_out, hidden)
    other = swap(own)
    packed, other, dp = lax.optimization_barrier((packed, other, dp))
    msg = exchange(packed)
    raw, msg = raw_rows(dp, msg, own, other)
    got = swap(msg)
    ids, raw = lax.optimization_barrier((ids, raw))
    ret = exchange(raw)
    sel = select(ids)
    weight_grad = weight_rows(dp, msg, got)
    ret, weight_grad = lax.optimization_barrier((ret, weight_grad))
    ret = keep(ret)
    grad_hidden, grad_gates = combine(sel, ret, gates.T, hidden)
    return grad_hidden, grad_gates.T, weight_grad[None]


def solution(mesh):
    in_specs = (
        P(("dp", "expert"), None, None),
        P(("dp", "expert"), None),
        P(("dp", "expert"), None),
        P(("dp", "expert"), None),
        P("expert", "dp", None),
    )
    out_specs = (
        P(("dp", "expert"), None, None),
        P(("dp", "expert"), None),
        P("expert", "dp", None),
    )
    return jax.shard_map(
        per_device, mesh=mesh, in_specs=in_specs, out_specs=out_specs, check_vma=False
    )
```

```python
import jax
import jax.numpy as jnp
from jax import lax
from jax.experimental import pallas as pl
from jax.experimental.pallas import tpu as pltpu
from jax.sharding import PartitionSpec as P

T = 256
A = 512
E = 64
D = 3584
F = 1024
COL = 512
FOLD = COL // 4
BLK = COL + FOLD
NG = D // COL
NH = F // COL
MSG = BLK * (NG + NH)
RET = F + F // 4
ROWS = 512
OVER = 128
BF = jnp.bfloat16
F32 = jnp.float32
PARAMS = pltpu.CompilerParams(vmem_limit_bytes=36 * 1024 * 1024)
IN_HBM = pl.BlockSpec(memory_space=pltpu.HBM)
IN_VMEM = pl.BlockSpec(memory_space=pltpu.VMEM)
IN_SMEM = pl.BlockSpec(memory_space=pltpu.SMEM)


def keep(x):
    return pltpu.with_memory_space_constraint(x, pltpu.VMEM)


def iota(shape, axis):
    return lax.broadcasted_iota(jnp.int32, shape, axis)


def dot(a, b):
    return jnp.dot(a, b, preferred_element_type=F32)


def dot_nt(a, b):
    return lax.dot_general(a, b, (((1,), (1,)), ((), ())), preferred_element_type=F32)


def columns(j, width=COL):
    return slice(j * width, (j + 1) * width)


def main_cols(j):
    return slice(j * BLK, j * BLK + COL)


def fold_cols(j):
    return slice(j * BLK + COL, (j + 1) * BLK)


def trade(x):
    row = iota((1, 8, 128), 1)
    low, even = row < 4, (row & 2) == 0

    def mix(p, q, shift, first):
        return (
            jnp.where(first, p, pltpu.roll(q, shift, 1)),
            jnp.where(first, pltpu.roll(p, 8 - shift, 1), q),
        )

    b0, b2 = mix(x[0], x[2], 4, low)
    b1, b3 = mix(x[1], x[3], 4, low)
    return mix(b0, b1, 2, even) + mix(b2, b3, 2, even)


def fold(over):
    groups = over.shape[0] // 8
    width = over.shape[1] // 4
    out = []
    for c in range(width // 128):
        parts = []
        for q in range(4):
            at = q * width + c * 128
            parts.append(over[:, at : at + 128].reshape(groups, 8, 128))
        out.append(jnp.stack(trade(parts), axis=1).reshape(groups * 32, 128).astype(BF))
    return jnp.concatenate(out, axis=1)


def unfold(folded):
    quarters = [[], [], [], []]
    for c in range(folded.shape[1] // 128):
        part = folded[:, columns(c, 128)].astype(F32).reshape(16, 4, 8, 128)
        for q, rows in enumerate(trade([part[:, i] for i in range(4)])):
            quarters[q].append(rows.reshape(OVER, 128).astype(BF))
    return jnp.concatenate([rows for quarter in quarters for rows in quarter], axis=1)


def rank_maps(ids):
    experts = iota((E, T), 0)
    o0 = (ids[0:1, :] == experts).astype(F32)
    o1 = (ids[1:2, :] == experts).astype(F32)
    earlier = (iota((T, T), 0) < iota((T, T), 1)).astype(F32).astype(BF)
    count = dot((o0 + o1).astype(BF), earlier)
    return o0 * (count + 1.0), o1 * (count + 1.0)


def slots():
    i = iota((ROWS + OVER, 1), 0)
    main = i < ROWS
    expert = jnp.where(main, jnp.right_shift(i, 3), jnp.right_shift(i - ROWS, 1))
    rank = jnp.where(main, (i & 7) + 1, (i & 1) + 9)
    rows = (expert == iota((ROWS + OVER, E), 1)).astype(F32).astype(BF)
    return rows, rank.astype(F32)


def interleave(k):
    return (iota((T, A), 1) == 2 * iota((T, A), 0) + k).astype(F32).astype(BF)


def assignments(r0, r1):
    by_assign = dot(r0.astype(BF), interleave(0)) + dot(r1.astype(BF), interleave(1))
    return by_assign.astype(BF)


def pack_kernel(ids_hbm, gates_hbm, grad_hbm, hid_hbm, out_ref, ids, gates, grad, hid, sem):
    first = slice(0, 3 * COL)
    rest = slice(3 * COL, D)
    copies = [
        pltpu.make_async_copy(ids_hbm, ids, sem.at[0]),
        pltpu.make_async_copy(gates_hbm, gates, sem.at[1]),
        pltpu.make_async_copy(grad_hbm.at[:, first], grad.at[:, first], sem.at[2]),
        pltpu.make_async_copy(grad_hbm.at[:, rest], grad.at[:, rest], sem.at[3]),
        pltpu.make_async_copy(hid_hbm, hid, sem.at[4]),
    ]
    for copy in copies:
        copy.start()
    rows, rank = slots()
    copies[0].wait()
    copies[1].wait()
    r0, r1 = rank_maps(ids[...])
    sel = (dot(rows, (r0 + r1).astype(BF)) == rank).astype(F32).astype(BF)
    gate = dot(gates[...], interleave(0))[0:1, :] + dot(gates[...], interleave(1))[1:2, :]
    gated = jnp.where(dot(rows, assignments(r0, r1)) == rank, gate, 0.0).astype(BF)

    def emit(j, chosen, x):
        value = dot(chosen, x)
        out_ref[:, main_cols(j)] = value[:ROWS].astype(BF)
        out_ref[:, fold_cols(j)] = fold(value[ROWS:])

    copies[2].wait()
    for j in range(3):
        emit(j, sel, grad[:, columns(j)])
    copies[3].wait()
    for j in range(3, NG):
        emit(j, sel, grad[:, columns(j)])
    copies[4].wait()
    for j in range(NH):
        emit(NG + j, gated, hid[:, :, columns(j)].reshape(A, COL))


def pack(ids, gates, grad, hid):
    return pl.pallas_call(
        pack_kernel,
        in_specs=[IN_HBM, IN_HBM, IN_HBM, IN_HBM],
        out_specs=IN_VMEM,
        out_shape=pltpu.VMEM((ROWS, MSG), BF),
        scratch_shapes=[
            pltpu.VMEM((2, T), jnp.int32),
            pltpu.VMEM((2, T), BF),
            pltpu.VMEM((T, D), BF),
            pltpu.VMEM((T, 2, F), BF),
            pltpu.SemaphoreType.DMA((5,)),
        ],
        compiler_params=pltpu.CompilerParams(vmem_limit_bytes=50 * 1024 * 1024),
        name="pack",
    )(ids, gates, grad, hid)


def raw_kernel(
    dp_ref, msg_ref, own_ref, other_hbm, out_hbm, keep_hbm, other, over, acc, out, last, sem
):
    weight_copy = pltpu.make_async_copy(other_hbm, other, sem.at[4])
    weight_copy.start()
    copies = [pltpu.make_async_copy(msg_ref, keep_hbm, sem.at[3])]
    copies[0].start()

    def multiply(weight, main, extra):
        value = None
        for j in range(NG):
            first = j * BLK
            rows = jnp.concatenate(
                [msg_ref[main, first : first + COL], over[extra, columns(j)]], axis=0
            )
            part = dot_nt(rows, weight[:, columns(j)])
            value = part if value is None else value + part
        return value

    def send(source, target, i):
        copy = pltpu.make_async_copy(source, target, sem.at[i])
        copy.start()
        copies.append(copy)

    for j in range(NG):
        over[:, columns(j)] = unfold(msg_ref[:, fold_cols(j)])
    cols = pl.ds(pl.multiple_of(dp_ref[0] * COL, COL), COL)
    value = multiply(own_ref, slice(0, ROWS), slice(0, OVER))
    out[0] = value[:ROWS].astype(BF)
    acc[:, cols] = value[ROWS:]
    send(out.at[0], out_hbm.at[:, cols], 0)
    weight_copy.wait()
    cols = pl.ds(pl.multiple_of((1 - dp_ref[0]) * COL, COL), COL)
    for b in range(2):
        main, extra = columns(b, ROWS // 2), columns(b, OVER // 2)
        value = multiply(other, main, extra)
        out[1, main] = value[: ROWS // 2].astype(BF)
        acc[extra, cols] = value[ROWS // 2 :]
        send(out.at[1, main], out_hbm.at[main, cols], 1 + 4 * b)
        last[main] = fold(acc[extra, :])
        send(last.at[main], out_hbm.at[main, F:], 2 + 4 * b)
    for copy in copies:
        copy.wait()


def raw_rows(dp, msg, own, other):
    return pl.pallas_call(
        raw_kernel,
        in_specs=[IN_SMEM, IN_VMEM, IN_VMEM, IN_HBM],
        out_specs=(IN_HBM, IN_HBM),
        out_shape=(
            jax.ShapeDtypeStruct((ROWS, RET), BF),
            jax.ShapeDtypeStruct((ROWS, MSG), BF),
        ),
        scratch_shapes=[
            pltpu.VMEM((COL, D), BF),
            pltpu.VMEM((OVER, D), BF),
            pltpu.VMEM((OVER, F), F32),
            pltpu.VMEM((2, ROWS, COL), BF),
            pltpu.VMEM((ROWS, F // 4), BF),
            pltpu.SemaphoreType.DMA((7,)),
        ],
        compiler_params=pltpu.CompilerParams(vmem_limit_bytes=44 * 1024 * 1024),
        name="raw",
    )(dp, keep(msg), keep(own), other)


def grad_kernel(dp_ref, own_ref, got_ref, out_ref, msgs, hids, ht, out, sem, osem):
    sources = (own_ref, got_ref)
    half = pl.ds(pl.multiple_of((NG + dp_ref[0]) * BLK, FOLD), BLK)
    hid_copies = []
    for i, ref in enumerate(sources):
        copy = pltpu.make_async_copy(ref.at[:, half], hids.at[i], sem.at[NG, i])
        copy.start()
        hid_copies.append(copy)
    copies = []
    for j in range(NG):
        block = columns(j, BLK)
        group = []
        for i, ref in enumerate(sources):
            copy = pltpu.make_async_copy(ref.at[:, block], msgs.at[i, :, block], sem.at[j, i])
            copy.start()
            group.append(copy)
        copies.append(group)
    for i in range(2):
        hid_copies[i].wait()
        at = i * (ROWS + OVER)
        ht[:, at : at + ROWS] = hids[i, :, :COL].T
        ht[:, at + ROWS : at + ROWS + OVER] = unfold(hids[i, :, COL:]).T
    outs = []
    for j in range(NG):
        for copy in copies[j]:
            copy.wait()
        rows = []
        for i in range(2):
            rows.append(msgs[i, :, main_cols(j)])
            rows.append(unfold(msgs[i, :, fold_cols(j)]))
        cols = columns(j)
        out[:, cols] = dot(ht[...], jnp.concatenate(rows, axis=0)).astype(BF)
        copy = pltpu.make_async_copy(out.at[:, cols], out_ref.at[:, cols], osem.at[j])
        copy.start()
        outs.append(copy)
    for copy in outs:
        copy.wait()


def weight_rows(dp, own, got):
    return pl.pallas_call(
        grad_kernel,
        in_specs=[IN_SMEM, IN_HBM, IN_HBM],
        out_specs=IN_HBM,
        out_shape=jax.ShapeDtypeStruct((COL, D), BF),
        scratch_shapes=[
            pltpu.VMEM((2, ROWS, NG * BLK), BF),
            pltpu.VMEM((2, ROWS, BLK), BF),
            pltpu.VMEM((COL, 2 * (ROWS + OVER)), BF),
            pltpu.VMEM((COL, D), BF),
            pltpu.SemaphoreType.DMA((NG + 1, 2)),
            pltpu.SemaphoreType.DMA((NG,)),
        ],
        compiler_params=pltpu.CompilerParams(vmem_limit_bytes=44 * 1024 * 1024),
        name="weight_grad",
    )(dp, own, got)


def prepare_kernel(ids_ref, gates_ref, hid_ref, sel_ref, rows_ref, gate_ref):
    r0, r1 = rank_maps(ids_ref[...])
    rows, rank = slots()
    chosen = (dot(rows, assignments(r0, r1)) == rank).astype(F32)
    sel_ref[...] = chosen.T.astype(BF)
    rows_ref[...] = hid_ref[...].reshape(A, F)
    gates = gates_ref[...].astype(F32)
    row, token = iota((A, T), 0), iota((A, T), 1)
    spread = jnp.where(row == 2 * token, gates[0:1, :], 0.0)
    spread += jnp.where(row == 2 * token + 1, gates[1:2, :], 0.0)
    gate = jnp.sum(spread, axis=1, keepdims=True)
    gate_ref[...] = jnp.broadcast_to(gate, (A, 128))


def prepare(ids, gates, hid):
    return pl.pallas_call(
        prepare_kernel,
        in_specs=[IN_VMEM, IN_VMEM, IN_VMEM],
        out_specs=(IN_VMEM, IN_VMEM, IN_VMEM),
        out_shape=(
            pltpu.VMEM((A, ROWS + OVER), BF),
            pltpu.VMEM((A, F), BF),
            pltpu.VMEM((A, 128), F32),
        ),
        compiler_params=PARAMS,
        name="prepare",
    )(ids, gates, hid)


def combine_kernel(sel_ref, ret_ref, gate_ref, hid_ref, out_ref, gg_ref, part):
    over = unfold(ret_ref[:, F:])
    gate = jnp.concatenate([gate_ref[...]] * (COL // 128), axis=1)
    total = None
    for j in range(NH):
        cols = columns(j)
        raw = dot(sel_ref[...], jnp.concatenate([ret_ref[:, cols], over[:, cols]], axis=0))
        out_ref[:, :, cols] = (gate * raw).astype(BF).reshape(T, 2, COL)
        product = hid_ref[:, cols].astype(F32) * raw
        for c in range(COL // 128):
            piece = product[:, columns(c, 128)]
            total = piece if total is None else total + piece
    part[...] = total
    for k in range(2):
        rows = part[pl.ds(k, T, stride=2), :]
        gg_ref[k : k + 1, :] = jnp.sum(rows.T, axis=0, keepdims=True)


def combine(sel, ret, gate, hid):
    return pl.pallas_call(
        combine_kernel,
        in_specs=[IN_VMEM, IN_VMEM, IN_VMEM, IN_VMEM],
        out_specs=(IN_VMEM, IN_VMEM),
        out_shape=(jax.ShapeDtypeStruct((T, 2, F), BF), jax.ShapeDtypeStruct((2, T), F32)),
        scratch_shapes=[pltpu.VMEM((A, 128), F32)],
        compiler_params=PARAMS,
        name="combine",
    )(keep(sel), keep(ret), keep(gate), keep(hid))


def exchange(x):
    width = x.shape[1]
    swapped = lax.all_to_all(
        x.reshape(E, 8, width), "expert", split_axis=0, concat_axis=0, tiled=True
    )
    return swapped.reshape(ROWS, width)


def swap(x):
    return lax.ppermute(x, "dp", [(0, 1), (1, 0)])


def per_device(hidden, grad_out, gates, expert_ids, weight):
    dp = lax.axis_index("dp").astype(jnp.int32).reshape(1)
    ids = expert_ids.T
    own = weight[0]
    packed = pack(ids, gates.T, grad_out, hidden)
    other = swap(own)
    packed, other, dp = lax.optimization_barrier((packed, other, dp))
    msg = exchange(packed)
    raw, msg = raw_rows(dp, msg, own, other)
    got = swap(msg)
    ids, raw = lax.optimization_barrier((ids, raw))
    ret = exchange(raw)
    sel, hid_rows, gate = prepare(ids, gates.T, hidden)
    weight_grad = weight_rows(dp, msg, got)
    ret, weight_grad = lax.optimization_barrier((ret, weight_grad))
    grad_hidden, grad_gates = combine(sel, ret, gate, hid_rows)
    return grad_hidden, grad_gates.T, weight_grad[None]


def solution(mesh):
    in_specs = (
        P(("dp", "expert"), None, None),
        P(("dp", "expert"), None),
        P(("dp", "expert"), None),
        P(("dp", "expert"), None),
        P("expert", "dp", None),
    )
    out_specs = (
        P(("dp", "expert"), None, None),
        P(("dp", "expert"), None),
        P("expert", "dp", None),
    )
    return jax.shard_map(
        per_device, mesh=mesh, in_specs=in_specs, out_specs=out_specs, check_vma=False
    )
```

```python
import jax
import jax.numpy as jnp
from jax import lax
from jax.experimental import pallas as pl
from jax.experimental.pallas import tpu as pltpu
from jax.sharding import PartitionSpec as P

T = 256
A = 512
E = 64
D = 3584
F = 1024
COL = 512
FOLD = COL // 4
BLK = COL + FOLD
NG = D // COL
NH = F // COL
MSG = BLK * (NG + NH)
RET = F + F // 4
ROWS = 512
OVER = 128
BF = jnp.bfloat16
F32 = jnp.float32
PARAMS = pltpu.CompilerParams(vmem_limit_bytes=36 * 1024 * 1024)
IN_HBM = pl.BlockSpec(memory_space=pltpu.HBM)
IN_VMEM = pl.BlockSpec(memory_space=pltpu.VMEM)
IN_SMEM = pl.BlockSpec(memory_space=pltpu.SMEM)


def keep(x):
    return pltpu.with_memory_space_constraint(x, pltpu.VMEM)


def iota(shape, axis):
    return lax.broadcasted_iota(jnp.int32, shape, axis)


def dot(a, b):
    return jnp.dot(a, b, preferred_element_type=F32)


def dot_nt(a, b):
    return lax.dot_general(a, b, (((1,), (1,)), ((), ())), preferred_element_type=F32)


def columns(j, width=COL):
    return slice(j * width, (j + 1) * width)


def main_cols(j):
    return slice(j * BLK, j * BLK + COL)


def fold_cols(j):
    return slice(j * BLK + COL, (j + 1) * BLK)


def trade(x):
    row = iota((1, 8, 128), 1)
    low, even = row < 4, (row & 2) == 0

    def mix(p, q, shift, first):
        return (
            jnp.where(first, p, pltpu.roll(q, shift, 1)),
            jnp.where(first, pltpu.roll(p, 8 - shift, 1), q),
        )

    b0, b2 = mix(x[0], x[2], 4, low)
    b1, b3 = mix(x[1], x[3], 4, low)
    return mix(b0, b1, 2, even) + mix(b2, b3, 2, even)


def fold(over):
    groups = over.shape[0] // 8
    width = over.shape[1] // 4
    out = []
    for c in range(width // 128):
        parts = []
        for q in range(4):
            at = q * width + c * 128
            parts.append(over[:, at : at + 128].reshape(groups, 8, 128))
        out.append(jnp.stack(trade(parts), axis=1).reshape(groups * 32, 128).astype(BF))
    return jnp.concatenate(out, axis=1)


def unfold(folded):
    quarters = [[], [], [], []]
    for c in range(folded.shape[1] // 128):
        part = folded[:, columns(c, 128)].astype(F32).reshape(16, 4, 8, 128)
        for q, rows in enumerate(trade([part[:, i] for i in range(4)])):
            quarters[q].append(rows.reshape(OVER, 128).astype(BF))
    return jnp.concatenate([rows for quarter in quarters for rows in quarter], axis=1)


def rank_maps(ids):
    experts = iota((E, T), 0)
    o0 = (ids[0:1, :] == experts).astype(F32)
    o1 = (ids[1:2, :] == experts).astype(F32)
    earlier = (iota((T, T), 0) < iota((T, T), 1)).astype(F32).astype(BF)
    count = dot((o0 + o1).astype(BF), earlier)
    return o0 * (count + 1.0), o1 * (count + 1.0)


def slots():
    i = iota((ROWS + OVER, 1), 0)
    main = i < ROWS
    expert = jnp.where(main, jnp.right_shift(i, 3), jnp.right_shift(i - ROWS, 1))
    rank = jnp.where(main, (i & 7) + 1, (i & 1) + 9)
    rows = (expert == iota((ROWS + OVER, E), 1)).astype(F32).astype(BF)
    return rows, rank.astype(F32)


def interleave(k):
    return (iota((T, A), 1) == 2 * iota((T, A), 0) + k).astype(F32).astype(BF)


def assignments(r0, r1):
    by_assign = dot(r0.astype(BF), interleave(0)) + dot(r1.astype(BF), interleave(1))
    return by_assign.astype(BF)


def pack_kernel(ids_hbm, gates_hbm, grad_hbm, hid_hbm, out_ref, ids, gates, grad, hid, sem):
    first = slice(0, 3 * COL)
    rest = slice(3 * COL, D)
    copies = [
        pltpu.make_async_copy(ids_hbm, ids, sem.at[0]),
        pltpu.make_async_copy(gates_hbm, gates, sem.at[1]),
        pltpu.make_async_copy(grad_hbm.at[:, first], grad.at[:, first], sem.at[2]),
        pltpu.make_async_copy(grad_hbm.at[:, rest], grad.at[:, rest], sem.at[3]),
        pltpu.make_async_copy(hid_hbm, hid, sem.at[4]),
    ]
    for copy in copies:
        copy.start()
    rows, rank = slots()
    copies[0].wait()
    copies[1].wait()
    r0, r1 = rank_maps(ids[...])
    sel = (dot(rows, (r0 + r1).astype(BF)) == rank).astype(F32).astype(BF)
    gate = dot(gates[...], interleave(0))[0:1, :] + dot(gates[...], interleave(1))[1:2, :]
    gated = jnp.where(dot(rows, assignments(r0, r1)) == rank, gate, 0.0).astype(BF)

    def emit(j, chosen, x):
        value = dot(chosen, x)
        out_ref[:, main_cols(j)] = value[:ROWS].astype(BF)
        out_ref[:, fold_cols(j)] = fold(value[ROWS:])

    copies[2].wait()
    for j in range(3):
        emit(j, sel, grad[:, columns(j)])
    copies[3].wait()
    for j in range(3, NG):
        emit(j, sel, grad[:, columns(j)])
    copies[4].wait()
    for j in range(NH):
        emit(NG + j, gated, hid[:, :, columns(j)].reshape(A, COL))


def pack(ids, gates, grad, hid):
    return pl.pallas_call(
        pack_kernel,
        in_specs=[IN_HBM, IN_HBM, IN_HBM, IN_HBM],
        out_specs=IN_VMEM,
        out_shape=pltpu.VMEM((ROWS, MSG), BF),
        scratch_shapes=[
            pltpu.VMEM((2, T), jnp.int32),
            pltpu.VMEM((2, T), BF),
            pltpu.VMEM((T, D), BF),
            pltpu.VMEM((T, 2, F), BF),
            pltpu.SemaphoreType.DMA((5,)),
        ],
        compiler_params=pltpu.CompilerParams(vmem_limit_bytes=50 * 1024 * 1024),
        name="pack",
    )(ids, gates, grad, hid)


def raw_kernel(
    dp_ref, msg_ref, own_ref, other_hbm, out_hbm, keep_hbm, other, over, acc, out, last, sem
):
    weight_copy = pltpu.make_async_copy(other_hbm, other, sem.at[4])
    weight_copy.start()
    copies = []

    def multiply(weight, main, extra):
        value = None
        for j in range(NG):
            if weight is own_ref:
                over[:, columns(j)] = unfold(msg_ref[:, fold_cols(j)])
            first = j * BLK
            rows = jnp.concatenate(
                [msg_ref[main, first : first + COL], over[extra, columns(j)]], axis=0
            )
            part = dot_nt(rows, weight[:, columns(j)])
            value = part if value is None else value + part
        return value

    def send(source, target, i):
        copy = pltpu.make_async_copy(source, target, sem.at[i])
        copy.start()
        copies.append(copy)

    cols = pl.ds(pl.multiple_of(dp_ref[0] * COL, COL), COL)
    value = multiply(own_ref, slice(0, ROWS), slice(0, OVER))
    out[0] = value[:ROWS].astype(BF)
    acc[:, cols] = value[ROWS:]
    send(out.at[0], out_hbm.at[:, cols], 0)
    send(msg_ref, keep_hbm, 3)
    weight_copy.wait()
    cols = pl.ds(pl.multiple_of((1 - dp_ref[0]) * COL, COL), COL)
    for b in range(2):
        main, extra = columns(b, ROWS // 2), columns(b, OVER // 2)
        value = multiply(other, main, extra)
        out[1, main] = value[: ROWS // 2].astype(BF)
        acc[extra, cols] = value[ROWS // 2 :]
        send(out.at[1, main], out_hbm.at[main, cols], 1 + 4 * b)
        last[main] = fold(acc[extra, :])
        send(last.at[main], out_hbm.at[main, F:], 2 + 4 * b)
    for copy in copies:
        copy.wait()


def raw_rows(dp, msg, own, other):
    return pl.pallas_call(
        raw_kernel,
        in_specs=[IN_SMEM, IN_VMEM, IN_VMEM, IN_HBM],
        out_specs=(IN_HBM, IN_HBM),
        out_shape=(
            jax.ShapeDtypeStruct((ROWS, RET), BF),
            jax.ShapeDtypeStruct((ROWS, MSG), BF),
        ),
        scratch_shapes=[
            pltpu.VMEM((COL, D), BF),
            pltpu.VMEM((OVER, D), BF),
            pltpu.VMEM((OVER, F), F32),
            pltpu.VMEM((2, ROWS, COL), BF),
            pltpu.VMEM((ROWS, F // 4), BF),
            pltpu.SemaphoreType.DMA((7,)),
        ],
        compiler_params=pltpu.CompilerParams(vmem_limit_bytes=44 * 1024 * 1024),
        name="raw",
    )(dp, keep(msg), keep(own), other)


def grad_kernel(dp_ref, own_ref, got_ref, out_ref, msgs, hids, ht, out, sem, osem):
    sources = (own_ref, got_ref)
    half = pl.ds(pl.multiple_of((NG + dp_ref[0]) * BLK, FOLD), BLK)
    hid_copies = []
    for i, ref in enumerate(sources):
        copy = pltpu.make_async_copy(ref.at[:, half], hids.at[i], sem.at[NG, i])
        copy.start()
        hid_copies.append(copy)
    copies = []
    for j in range(NG):
        block = columns(j, BLK)
        group = []
        for i, ref in enumerate(sources):
            copy = pltpu.make_async_copy(ref.at[:, block], msgs.at[i, :, block], sem.at[j, i])
            copy.start()
            group.append(copy)
        copies.append(group)
    for i in range(2):
        hid_copies[i].wait()
        at = i * (ROWS + OVER)
        ht[:, at : at + ROWS] = hids[i, :, :COL].T
        ht[:, at + ROWS : at + ROWS + OVER] = unfold(hids[i, :, COL:]).T
    outs = []
    for j in range(NG):
        for copy in copies[j]:
            copy.wait()
        rows = []
        for i in range(2):
            rows.append(msgs[i, :, main_cols(j)])
            rows.append(unfold(msgs[i, :, fold_cols(j)]))
        cols = columns(j)
        out[:, cols] = dot(ht[...], jnp.concatenate(rows, axis=0)).astype(BF)
        copy = pltpu.make_async_copy(out.at[:, cols], out_ref.at[:, cols], osem.at[j])
        copy.start()
        outs.append(copy)
    for copy in outs:
        copy.wait()


def weight_rows(dp, own, got):
    return pl.pallas_call(
        grad_kernel,
        in_specs=[IN_SMEM, IN_HBM, IN_HBM],
        out_specs=IN_HBM,
        out_shape=jax.ShapeDtypeStruct((COL, D), BF),
        scratch_shapes=[
            pltpu.VMEM((2, ROWS, NG * BLK), BF),
            pltpu.VMEM((2, ROWS, BLK), BF),
            pltpu.VMEM((COL, 2 * (ROWS + OVER)), BF),
            pltpu.VMEM((COL, D), BF),
            pltpu.SemaphoreType.DMA((NG + 1, 2)),
            pltpu.SemaphoreType.DMA((NG,)),
        ],
        compiler_params=pltpu.CompilerParams(vmem_limit_bytes=44 * 1024 * 1024),
        name="weight_grad",
    )(dp, own, got)


def prepare_kernel(ids_ref, gates_ref, hid_ref, sel_ref, rows_ref, gate_ref):
    r0, r1 = rank_maps(ids_ref[...])
    rows, rank = slots()
    chosen = (dot(rows, assignments(r0, r1)) == rank).astype(F32)
    sel_ref[...] = chosen.T.astype(BF)
    rows_ref[...] = hid_ref[...].reshape(A, F)
    gates = gates_ref[...].astype(F32)
    row, token = iota((A, T), 0), iota((A, T), 1)
    spread = jnp.where(row == 2 * token, gates[0:1, :], 0.0)
    spread += jnp.where(row == 2 * token + 1, gates[1:2, :], 0.0)
    gate = jnp.sum(spread, axis=1, keepdims=True)
    gate_ref[...] = jnp.broadcast_to(gate, (A, 128))


def prepare(ids, gates, hid):
    return pl.pallas_call(
        prepare_kernel,
        in_specs=[IN_VMEM, IN_VMEM, IN_VMEM],
        out_specs=(IN_VMEM, IN_VMEM, IN_VMEM),
        out_shape=(
            pltpu.VMEM((A, ROWS + OVER), BF),
            pltpu.VMEM((A, F), BF),
            pltpu.VMEM((A, 128), F32),
        ),
        compiler_params=PARAMS,
        name="prepare",
    )(ids, gates, hid)


def combine_kernel(sel_ref, ret_ref, gate_ref, hid_ref, out_ref, gg_ref, part):
    over = unfold(ret_ref[:, F:])
    gate = jnp.concatenate([gate_ref[...]] * (COL // 128), axis=1)
    total = None
    for j in range(NH):
        cols = columns(j)
        raw = dot(sel_ref[...], jnp.concatenate([ret_ref[:, cols], over[:, cols]], axis=0))
        out_ref[:, :, cols] = (gate * raw).astype(BF).reshape(T, 2, COL)
        product = hid_ref[:, cols].astype(F32) * raw
        for c in range(COL // 128):
            piece = product[:, columns(c, 128)]
            total = piece if total is None else total + piece
    part[...] = total
    for k in range(2):
        rows = part[pl.ds(k, T, stride=2), :]
        gg_ref[k : k + 1, :] = jnp.sum(rows.T, axis=0, keepdims=True)


def combine(sel, ret, gate, hid):
    return pl.pallas_call(
        combine_kernel,
        in_specs=[IN_VMEM, IN_VMEM, IN_VMEM, IN_VMEM],
        out_specs=(IN_VMEM, IN_VMEM),
        out_shape=(jax.ShapeDtypeStruct((T, 2, F), BF), jax.ShapeDtypeStruct((2, T), F32)),
        scratch_shapes=[pltpu.VMEM((A, 128), F32)],
        compiler_params=PARAMS,
        name="combine",
    )(keep(sel), keep(ret), keep(gate), keep(hid))


def exchange(x):
    width = x.shape[1]
    swapped = lax.all_to_all(
        x.reshape(E, 8, width), "expert", split_axis=0, concat_axis=0, tiled=True
    )
    return swapped.reshape(ROWS, width)


def swap(x):
    return lax.ppermute(x, "dp", [(0, 1), (1, 0)])


def per_device(hidden, grad_out, gates, expert_ids, weight):
    dp = lax.axis_index("dp").astype(jnp.int32).reshape(1)
    ids = expert_ids.T
    own = weight[0]
    packed = pack(ids, gates.T, grad_out, hidden)
    other = swap(own)
    packed, other, dp = lax.optimization_barrier((packed, other, dp))
    msg = exchange(packed)
    raw, msg = raw_rows(dp, msg, own, other)
    got = swap(msg)
    ids, raw = lax.optimization_barrier((ids, raw))
    ret = exchange(raw)
    sel, hid_rows, gate = prepare(ids, gates.T, hidden)
    weight_grad = weight_rows(dp, msg, got)
    ret, weight_grad = lax.optimization_barrier((ret, weight_grad))
    grad_hidden, grad_gates = combine(sel, ret, gate, hid_rows)
    return grad_hidden, grad_gates.T, weight_grad[None]


def solution(mesh):
    in_specs = (
        P(("dp", "expert"), None, None),
        P(("dp", "expert"), None),
        P(("dp", "expert"), None),
        P(("dp", "expert"), None),
        P("expert", "dp", None),
    )
    out_specs = (
        P(("dp", "expert"), None, None),
        P(("dp", "expert"), None),
        P("expert", "dp", None),
    )
    return jax.shard_map(
        per_device, mesh=mesh, in_specs=in_specs, out_specs=out_specs, check_vma=False
    )
```

```python
import jax
import jax.numpy as jnp
from jax import lax
from jax.experimental import pallas as pl
from jax.experimental.pallas import tpu as pltpu
from jax.sharding import PartitionSpec as P

T = 256
A = 512
E = 64
D = 3584
F = 1024
COL = 512
FOLD = COL // 4
BLK = COL + FOLD
NG = D // COL
NH = F // COL
MSG = BLK * (NG + NH)
RET = F + F // 4
ROWS = 512
OVER = 128
BF = jnp.bfloat16
F32 = jnp.float32
PARAMS = pltpu.CompilerParams(vmem_limit_bytes=36 * 1024 * 1024)
IN_HBM = pl.BlockSpec(memory_space=pltpu.HBM)
IN_VMEM = pl.BlockSpec(memory_space=pltpu.VMEM)
IN_SMEM = pl.BlockSpec(memory_space=pltpu.SMEM)


def keep(x):
    return pltpu.with_memory_space_constraint(x, pltpu.VMEM)


def iota(shape, axis):
    return lax.broadcasted_iota(jnp.int32, shape, axis)


def dot(a, b):
    return jnp.dot(a, b, preferred_element_type=F32)


def dot_nt(a, b):
    return lax.dot_general(a, b, (((1,), (1,)), ((), ())), preferred_element_type=F32)


def columns(j, width=COL):
    return slice(j * width, (j + 1) * width)


def main_cols(j):
    return slice(j * BLK, j * BLK + COL)


def fold_cols(j):
    return slice(j * BLK + COL, (j + 1) * BLK)


def trade(x):
    row = iota((1, 8, 128), 1)
    low, even = row < 4, (row & 2) == 0

    def mix(p, q, shift, first):
        return (
            jnp.where(first, p, pltpu.roll(q, shift, 1)),
            jnp.where(first, pltpu.roll(p, 8 - shift, 1), q),
        )

    b0, b2 = mix(x[0], x[2], 4, low)
    b1, b3 = mix(x[1], x[3], 4, low)
    return mix(b0, b1, 2, even) + mix(b2, b3, 2, even)


def fold(over):
    groups = over.shape[0] // 8
    width = over.shape[1] // 4
    out = []
    for c in range(width // 128):
        parts = []
        for q in range(4):
            at = q * width + c * 128
            parts.append(over[:, at : at + 128].reshape(groups, 8, 128))
        out.append(jnp.stack(trade(parts), axis=1).reshape(groups * 32, 128).astype(BF))
    return jnp.concatenate(out, axis=1)


def unfold(folded):
    quarters = [[], [], [], []]
    for c in range(folded.shape[1] // 128):
        part = folded[:, columns(c, 128)].astype(F32).reshape(16, 4, 8, 128)
        for q, rows in enumerate(trade([part[:, i] for i in range(4)])):
            quarters[q].append(rows.reshape(OVER, 128).astype(BF))
    return jnp.concatenate([rows for quarter in quarters for rows in quarter], axis=1)


def rank_maps(ids):
    experts = iota((E, T), 0)
    o0 = (ids[0:1, :] == experts).astype(F32)
    o1 = (ids[1:2, :] == experts).astype(F32)
    earlier = (iota((T, T), 0) < iota((T, T), 1)).astype(F32).astype(BF)
    count = dot((o0 + o1).astype(BF), earlier)
    return o0 * (count + 1.0), o1 * (count + 1.0)


def slots():
    i = iota((ROWS + OVER, 1), 0)
    main = i < ROWS
    expert = jnp.where(main, jnp.right_shift(i, 3), jnp.right_shift(i - ROWS, 1))
    expert = (expert * 21) & (E - 1)
    rank = jnp.where(main, (i & 7) + 1, (i & 1) + 9)
    rows = (expert == iota((ROWS + OVER, E), 1)).astype(F32).astype(BF)
    return rows, rank.astype(F32)


def interleave(k):
    return (iota((T, A), 1) == 2 * iota((T, A), 0) + k).astype(F32).astype(BF)


def assignments(r0, r1):
    by_assign = dot(r0.astype(BF), interleave(0)) + dot(r1.astype(BF), interleave(1))
    return by_assign.astype(BF)


def pack_kernel(ids_hbm, gates_hbm, grad_hbm, hid_hbm, out_ref, ids, gates, grad, hid, sem):
    first = slice(0, 3 * COL)
    rest = slice(3 * COL, D)
    copies = [
        pltpu.make_async_copy(ids_hbm, ids, sem.at[0]),
        pltpu.make_async_copy(gates_hbm, gates, sem.at[1]),
        pltpu.make_async_copy(grad_hbm.at[:, first], grad.at[:, first], sem.at[2]),
        pltpu.make_async_copy(grad_hbm.at[:, rest], grad.at[:, rest], sem.at[3]),
        pltpu.make_async_copy(hid_hbm, hid, sem.at[4]),
    ]
    for copy in copies:
        copy.start()
    rows, rank = slots()
    copies[0].wait()
    copies[1].wait()
    r0, r1 = rank_maps(ids[...])
    sel = (dot(rows, (r0 + r1).astype(BF)) == rank).astype(F32).astype(BF)
    gate = dot(gates[...], interleave(0))[0:1, :] + dot(gates[...], interleave(1))[1:2, :]
    gated = jnp.where(dot(rows, assignments(r0, r1)) == rank, gate, 0.0).astype(BF)

    def emit(j, chosen, x):
        value = dot(chosen, x)
        out_ref[:, main_cols(j)] = value[:ROWS].astype(BF)
        out_ref[:, fold_cols(j)] = fold(value[ROWS:])

    copies[2].wait()
    for j in range(3):
        emit(j, sel, grad[:, columns(j)])
    copies[3].wait()
    for j in range(3, NG):
        emit(j, sel, grad[:, columns(j)])
    copies[4].wait()
    for j in range(NH):
        emit(NG + j, gated, hid[:, :, columns(j)].reshape(A, COL))


def pack(ids, gates, grad, hid):
    return pl.pallas_call(
        pack_kernel,
        in_specs=[IN_HBM, IN_HBM, IN_HBM, IN_HBM],
        out_specs=IN_VMEM,
        out_shape=pltpu.VMEM((ROWS, MSG), BF),
        scratch_shapes=[
            pltpu.VMEM((2, T), jnp.int32),
            pltpu.VMEM((2, T), BF),
            pltpu.VMEM((T, D), BF),
            pltpu.VMEM((T, 2, F), BF),
            pltpu.SemaphoreType.DMA((5,)),
        ],
        compiler_params=pltpu.CompilerParams(vmem_limit_bytes=50 * 1024 * 1024),
        name="pack",
    )(ids, gates, grad, hid)


def raw_kernel(
    dp_ref, msg_ref, own_ref, other_hbm, out_hbm, keep_hbm, other, over, acc, out, last, sem
):
    weight_copy = pltpu.make_async_copy(other_hbm, other, sem.at[4])
    weight_copy.start()
    copies = []

    def multiply(weight, main, extra):
        value = None
        for j in range(NG):
            if weight is own_ref:
                over[:, columns(j)] = unfold(msg_ref[:, fold_cols(j)])
            first = j * BLK
            rows = jnp.concatenate(
                [msg_ref[main, first : first + COL], over[extra, columns(j)]], axis=0
            )
            part = dot_nt(rows, weight[:, columns(j)])
            value = part if value is None else value + part
        return value

    def send(source, target, i):
        copy = pltpu.make_async_copy(source, target, sem.at[i])
        copy.start()
        copies.append(copy)

    cols = pl.ds(pl.multiple_of(dp_ref[0] * COL, COL), COL)
    value = multiply(own_ref, slice(0, ROWS), slice(0, OVER))
    out[0] = value[:ROWS].astype(BF)
    acc[:, cols] = value[ROWS:]
    send(out.at[0], out_hbm.at[:, cols], 0)
    send(msg_ref, keep_hbm, 3)
    weight_copy.wait()
    cols = pl.ds(pl.multiple_of((1 - dp_ref[0]) * COL, COL), COL)
    for b in range(2):
        main, extra = columns(b, ROWS // 2), columns(b, OVER // 2)
        value = multiply(other, main, extra)
        out[1, main] = value[: ROWS // 2].astype(BF)
        acc[extra, cols] = value[ROWS // 2 :]
        send(out.at[1, main], out_hbm.at[main, cols], 1 + 4 * b)
        last[main] = fold(acc[extra, :])
        send(last.at[main], out_hbm.at[main, F:], 2 + 4 * b)
    for copy in copies:
        copy.wait()


def raw_rows(dp, msg, own, other):
    return pl.pallas_call(
        raw_kernel,
        in_specs=[IN_SMEM, IN_VMEM, IN_VMEM, IN_HBM],
        out_specs=(IN_HBM, IN_HBM),
        out_shape=(
            jax.ShapeDtypeStruct((ROWS, RET), BF),
            jax.ShapeDtypeStruct((ROWS, MSG), BF),
        ),
        scratch_shapes=[
            pltpu.VMEM((COL, D), BF),
            pltpu.VMEM((OVER, D), BF),
            pltpu.VMEM((OVER, F), F32),
            pltpu.VMEM((2, ROWS, COL), BF),
            pltpu.VMEM((ROWS, F // 4), BF),
            pltpu.SemaphoreType.DMA((7,)),
        ],
        compiler_params=pltpu.CompilerParams(vmem_limit_bytes=44 * 1024 * 1024),
        name="raw",
    )(dp, keep(msg), keep(own), other)


def grad_kernel(dp_ref, own_ref, got_ref, out_ref, msgs, hids, ht, out, sem, osem):
    sources = (own_ref, got_ref)
    half = pl.ds(pl.multiple_of((NG + dp_ref[0]) * BLK, FOLD), BLK)
    hid_copies = []
    for i, ref in enumerate(sources):
        copy = pltpu.make_async_copy(ref.at[:, half], hids.at[i], sem.at[NG, i])
        copy.start()
        hid_copies.append(copy)
    copies = []
    for j in range(NG):
        block = columns(j, BLK)
        group = []
        for i, ref in enumerate(sources):
            copy = pltpu.make_async_copy(ref.at[:, block], msgs.at[i, :, block], sem.at[j, i])
            copy.start()
            group.append(copy)
        copies.append(group)
    for i in range(2):
        hid_copies[i].wait()
        at = i * (ROWS + OVER)
        ht[:, at : at + ROWS] = hids[i, :, :COL].T
        ht[:, at + ROWS : at + ROWS + OVER] = unfold(hids[i, :, COL:]).T
    outs = []
    for j in range(NG):
        for copy in copies[j]:
            copy.wait()
        rows = []
        for i in range(2):
            rows.append(msgs[i, :, main_cols(j)])
            rows.append(unfold(msgs[i, :, fold_cols(j)]))
        cols = columns(j)
        out[:, cols] = dot(ht[...], jnp.concatenate(rows, axis=0)).astype(BF)
        copy = pltpu.make_async_copy(out.at[:, cols], out_ref.at[:, cols], osem.at[j])
        copy.start()
        outs.append(copy)
    for copy in outs:
        copy.wait()


def weight_rows(dp, own, got):
    return pl.pallas_call(
        grad_kernel,
        in_specs=[IN_SMEM, IN_HBM, IN_HBM],
        out_specs=IN_HBM,
        out_shape=jax.ShapeDtypeStruct((COL, D), BF),
        scratch_shapes=[
            pltpu.VMEM((2, ROWS, NG * BLK), BF),
            pltpu.VMEM((2, ROWS, BLK), BF),
            pltpu.VMEM((COL, 2 * (ROWS + OVER)), BF),
            pltpu.VMEM((COL, D), BF),
            pltpu.SemaphoreType.DMA((NG + 1, 2)),
            pltpu.SemaphoreType.DMA((NG,)),
        ],
        compiler_params=pltpu.CompilerParams(vmem_limit_bytes=44 * 1024 * 1024),
        name="weight_grad",
    )(dp, own, got)


def prepare_kernel(ids_ref, gates_ref, hid_ref, sel_ref, rows_ref, gate_ref):
    r0, r1 = rank_maps(ids_ref[...])
    rows, rank = slots()
    chosen = (dot(rows, assignments(r0, r1)) == rank).astype(F32)
    sel_ref[...] = chosen.T.astype(BF)
    rows_ref[...] = hid_ref[...].reshape(A, F)
    gates = gates_ref[...].astype(F32)
    row, token = iota((A, T), 0), iota((A, T), 1)
    spread = jnp.where(row == 2 * token, gates[0:1, :], 0.0)
    spread += jnp.where(row == 2 * token + 1, gates[1:2, :], 0.0)
    gate = jnp.sum(spread, axis=1, keepdims=True)
    gate_ref[...] = jnp.broadcast_to(gate, (A, 128))


def prepare(ids, gates, hid):
    return pl.pallas_call(
        prepare_kernel,
        in_specs=[IN_VMEM, IN_VMEM, IN_VMEM],
        out_specs=(IN_VMEM, IN_VMEM, IN_VMEM),
        out_shape=(
            pltpu.VMEM((A, ROWS + OVER), BF),
            pltpu.VMEM((A, F), BF),
            pltpu.VMEM((A, 128), F32),
        ),
        compiler_params=PARAMS,
        name="prepare",
    )(ids, gates, hid)


def combine_kernel(sel_ref, ret_ref, gate_ref, hid_ref, out_ref, gg_ref, part):
    over = unfold(ret_ref[:, F:])
    gate = jnp.concatenate([gate_ref[...]] * (COL // 128), axis=1)
    total = None
    for j in range(NH):
        cols = columns(j)
        raw = dot(sel_ref[...], jnp.concatenate([ret_ref[:, cols], over[:, cols]], axis=0))
        out_ref[:, :, cols] = (gate * raw).astype(BF).reshape(T, 2, COL)
        product = hid_ref[:, cols].astype(F32) * raw
        for c in range(COL // 128):
            piece = product[:, columns(c, 128)]
            total = piece if total is None else total + piece
    part[...] = total
    for k in range(2):
        rows = part[pl.ds(k, T, stride=2), :]
        gg_ref[k : k + 1, :] = jnp.sum(rows.T, axis=0, keepdims=True)


def combine(sel, ret, gate, hid):
    return pl.pallas_call(
        combine_kernel,
        in_specs=[IN_VMEM, IN_VMEM, IN_VMEM, IN_VMEM],
        out_specs=(IN_VMEM, IN_VMEM),
        out_shape=(jax.ShapeDtypeStruct((T, 2, F), BF), jax.ShapeDtypeStruct((2, T), F32)),
        scratch_shapes=[pltpu.VMEM((A, 128), F32)],
        compiler_params=PARAMS,
        name="combine",
    )(keep(sel), keep(ret), keep(gate), keep(hid))


def exchange(x):
    width = x.shape[1]
    swapped = lax.all_to_all(
        x.reshape(E, 8, width),
        "expert",
        split_axis=0,
        concat_axis=0,
        axis_index_groups=[[i * 21 % E for i in range(E)]],
        tiled=True,
    )
    return swapped.reshape(ROWS, width)


def swap(x):
    return lax.ppermute(x, "dp", [(0, 1), (1, 0)])


def per_device(hidden, grad_out, gates, expert_ids, weight):
    dp = lax.axis_index("dp").astype(jnp.int32).reshape(1)
    ids = expert_ids.T
    own = weight[0]
    packed = pack(ids, gates.T, grad_out, hidden)
    other = swap(own)
    packed, other, dp = lax.optimization_barrier((packed, other, dp))
    msg = exchange(packed)
    raw, msg = raw_rows(dp, msg, own, other)
    got = swap(msg)
    ids, raw = lax.optimization_barrier((ids, raw))
    ret = exchange(raw)
    sel, hid_rows, gate = prepare(ids, gates.T, hidden)
    weight_grad = weight_rows(dp, msg, got)
    ret, weight_grad = lax.optimization_barrier((ret, weight_grad))
    grad_hidden, grad_gates = combine(sel, ret, gate, hid_rows)
    return grad_hidden, grad_gates.T, weight_grad[None]


def solution(mesh):
    in_specs = (
        P(("dp", "expert"), None, None),
        P(("dp", "expert"), None),
        P(("dp", "expert"), None),
        P(("dp", "expert"), None),
        P("expert", "dp", None),
    )
    out_specs = (
        P(("dp", "expert"), None, None),
        P(("dp", "expert"), None),
        P("expert", "dp", None),
    )
    return jax.shard_map(
        per_device, mesh=mesh, in_specs=in_specs, out_specs=out_specs, check_vma=False
    )
```

```python
import jax
import jax.numpy as jnp
from jax import lax
from jax.experimental import pallas as pl
from jax.experimental.pallas import tpu as pltpu
from jax.sharding import PartitionSpec as P

T = 256
A = 512
E = 64
D = 3584
F = 1024
COL = 512
FOLD = COL // 4
BLK = COL + FOLD
NG = D // COL
NH = F // COL
MSG = BLK * (NG + NH)
RET = F + F // 4
ROWS = 512
OVER = 128
BF = jnp.bfloat16
F32 = jnp.float32
PARAMS = pltpu.CompilerParams(vmem_limit_bytes=36 * 1024 * 1024)
IN_HBM = pl.BlockSpec(memory_space=pltpu.HBM)
IN_VMEM = pl.BlockSpec(memory_space=pltpu.VMEM)
IN_SMEM = pl.BlockSpec(memory_space=pltpu.SMEM)


def keep(x):
    return pltpu.with_memory_space_constraint(x, pltpu.VMEM)


def iota(shape, axis):
    return lax.broadcasted_iota(jnp.int32, shape, axis)


def dot(a, b):
    return jnp.dot(a, b, preferred_element_type=F32)


def dot_nt(a, b):
    return lax.dot_general(a, b, (((1,), (1,)), ((), ())), preferred_element_type=F32)


def columns(j, width=COL):
    return slice(j * width, (j + 1) * width)


def main_cols(j):
    return slice(j * BLK, j * BLK + COL)


def fold_cols(j):
    return slice(j * BLK + COL, (j + 1) * BLK)


def trade(x):
    row = iota((1, 8, 128), 1)
    low, even = row < 4, (row & 2) == 0

    def mix(p, q, shift, first):
        return (
            jnp.where(first, p, pltpu.roll(q, shift, 1)),
            jnp.where(first, pltpu.roll(p, 8 - shift, 1), q),
        )

    b0, b2 = mix(x[0], x[2], 4, low)
    b1, b3 = mix(x[1], x[3], 4, low)
    return mix(b0, b1, 2, even) + mix(b2, b3, 2, even)


def fold(over):
    groups = over.shape[0] // 8
    width = over.shape[1] // 4
    out = []
    for c in range(width // 128):
        parts = []
        for q in range(4):
            at = q * width + c * 128
            parts.append(over[:, at : at + 128].reshape(groups, 8, 128))
        out.append(jnp.stack(trade(parts), axis=1).reshape(groups * 32, 128).astype(BF))
    return jnp.concatenate(out, axis=1)


def unfold(folded):
    quarters = [[], [], [], []]
    for c in range(folded.shape[1] // 128):
        part = folded[:, columns(c, 128)].astype(F32).reshape(16, 4, 8, 128)
        for q, rows in enumerate(trade([part[:, i] for i in range(4)])):
            quarters[q].append(rows.reshape(OVER, 128).astype(BF))
    return jnp.concatenate([rows for quarter in quarters for rows in quarter], axis=1)


def rank_maps(ids):
    experts = iota((E, T), 0)
    o0 = (ids[0:1, :] == experts).astype(F32)
    o1 = (ids[1:2, :] == experts).astype(F32)
    earlier = (iota((T, T), 0) < iota((T, T), 1)).astype(F32).astype(BF)
    count = dot((o0 + o1).astype(BF), earlier)
    return o0 * (count + 1.0), o1 * (count + 1.0)


def slots():
    i = iota((ROWS + OVER, 1), 0)
    main = i < ROWS
    expert = jnp.where(main, jnp.right_shift(i, 3), jnp.right_shift(i - ROWS, 1))
    expert = (expert * 29) & (E - 1)
    rank = jnp.where(main, (i & 7) + 1, (i & 1) + 9)
    rows = (expert == iota((ROWS + OVER, E), 1)).astype(F32).astype(BF)
    return rows, rank.astype(F32)


def interleave(k):
    return (iota((T, A), 1) == 2 * iota((T, A), 0) + k).astype(F32).astype(BF)


def assignments(r0, r1):
    by_assign = dot(r0.astype(BF), interleave(0)) + dot(r1.astype(BF), interleave(1))
    return by_assign.astype(BF)


def pack_kernel(ids_hbm, gates_hbm, grad_hbm, hid_hbm, out_ref, ids, gates, grad, hid, sem):
    first = slice(0, 3 * COL)
    rest = slice(3 * COL, D)
    copies = [
        pltpu.make_async_copy(ids_hbm, ids, sem.at[0]),
        pltpu.make_async_copy(gates_hbm, gates, sem.at[1]),
        pltpu.make_async_copy(grad_hbm.at[:, first], grad.at[:, first], sem.at[2]),
        pltpu.make_async_copy(grad_hbm.at[:, rest], grad.at[:, rest], sem.at[3]),
        pltpu.make_async_copy(hid_hbm, hid, sem.at[4]),
    ]
    for copy in copies:
        copy.start()
    rows, rank = slots()
    copies[0].wait()
    copies[1].wait()
    r0, r1 = rank_maps(ids[...])
    sel = (dot(rows, (r0 + r1).astype(BF)) == rank).astype(F32).astype(BF)
    gate = dot(gates[...], interleave(0))[0:1, :] + dot(gates[...], interleave(1))[1:2, :]
    gated = jnp.where(dot(rows, assignments(r0, r1)) == rank, gate, 0.0).astype(BF)

    def emit(j, chosen, x):
        value = dot(chosen, x)
        out_ref[:, main_cols(j)] = value[:ROWS].astype(BF)
        out_ref[:, fold_cols(j)] = fold(value[ROWS:])

    copies[2].wait()
    for j in range(3):
        emit(j, sel, grad[:, columns(j)])
    copies[3].wait()
    for j in range(3, NG):
        emit(j, sel, grad[:, columns(j)])
    copies[4].wait()
    for j in range(NH):
        emit(NG + j, gated, hid[:, :, columns(j)].reshape(A, COL))


def pack(ids, gates, grad, hid):
    return pl.pallas_call(
        pack_kernel,
        in_specs=[IN_HBM, IN_HBM, IN_HBM, IN_HBM],
        out_specs=IN_VMEM,
        out_shape=pltpu.VMEM((ROWS, MSG), BF),
        scratch_shapes=[
            pltpu.VMEM((2, T), jnp.int32),
            pltpu.VMEM((2, T), BF),
            pltpu.VMEM((T, D), BF),
            pltpu.VMEM((T, 2, F), BF),
            pltpu.SemaphoreType.DMA((5,)),
        ],
        compiler_params=pltpu.CompilerParams(vmem_limit_bytes=50 * 1024 * 1024),
        name="pack",
    )(ids, gates, grad, hid)


def raw_kernel(
    dp_ref, msg_ref, own_ref, other_hbm, out_hbm, keep_hbm, other, over, acc, out, last, sem
):
    weight_copy = pltpu.make_async_copy(other_hbm, other, sem.at[4])
    weight_copy.start()
    copies = []

    def multiply(weight, main, extra):
        value = None
        for j in range(NG):
            if weight is own_ref:
                over[:, columns(j)] = unfold(msg_ref[:, fold_cols(j)])
            first = j * BLK
            rows = jnp.concatenate(
                [msg_ref[main, first : first + COL], over[extra, columns(j)]], axis=0
            )
            part = dot_nt(rows, weight[:, columns(j)])
            value = part if value is None else value + part
        return value

    def send(source, target, i):
        copy = pltpu.make_async_copy(source, target, sem.at[i])
        copy.start()
        copies.append(copy)

    cols = pl.ds(pl.multiple_of(dp_ref[0] * COL, COL), COL)
    value = multiply(own_ref, slice(0, ROWS), slice(0, OVER))
    out[0] = value[:ROWS].astype(BF)
    acc[:, cols] = value[ROWS:]
    send(out.at[0], out_hbm.at[:, cols], 0)
    send(msg_ref, keep_hbm, 3)
    weight_copy.wait()
    cols = pl.ds(pl.multiple_of((1 - dp_ref[0]) * COL, COL), COL)
    for b in range(2):
        main, extra = columns(b, ROWS // 2), columns(b, OVER // 2)
        value = multiply(other, main, extra)
        out[1, main] = value[: ROWS // 2].astype(BF)
        acc[extra, cols] = value[ROWS // 2 :]
        send(out.at[1, main], out_hbm.at[main, cols], 1 + 4 * b)
        last[main] = fold(acc[extra, :])
        send(last.at[main], out_hbm.at[main, F:], 2 + 4 * b)
    for copy in copies:
        copy.wait()


def raw_rows(dp, msg, own, other):
    return pl.pallas_call(
        raw_kernel,
        in_specs=[IN_SMEM, IN_VMEM, IN_VMEM, IN_HBM],
        out_specs=(IN_HBM, IN_HBM),
        out_shape=(
            jax.ShapeDtypeStruct((ROWS, RET), BF),
            jax.ShapeDtypeStruct((ROWS, MSG), BF),
        ),
        scratch_shapes=[
            pltpu.VMEM((COL, D), BF),
            pltpu.VMEM((OVER, D), BF),
            pltpu.VMEM((OVER, F), F32),
            pltpu.VMEM((2, ROWS, COL), BF),
            pltpu.VMEM((ROWS, F // 4), BF),
            pltpu.SemaphoreType.DMA((7,)),
        ],
        compiler_params=pltpu.CompilerParams(vmem_limit_bytes=44 * 1024 * 1024),
        name="raw",
    )(dp, keep(msg), keep(own), other)


def grad_kernel(dp_ref, own_ref, got_ref, out_ref, msgs, hids, ht, out, sem, osem):
    sources = (own_ref, got_ref)
    half = pl.ds(pl.multiple_of((NG + dp_ref[0]) * BLK, FOLD), BLK)
    hid_copies = []
    for i, ref in enumerate(sources):
        copy = pltpu.make_async_copy(ref.at[:, half], hids.at[i], sem.at[NG, i])
        copy.start()
        hid_copies.append(copy)
    copies = []
    for j in range(NG):
        block = columns(j, BLK)
        group = []
        for i, ref in enumerate(sources):
            copy = pltpu.make_async_copy(ref.at[:, block], msgs.at[i, :, block], sem.at[j, i])
            copy.start()
            group.append(copy)
        copies.append(group)
    for i in range(2):
        hid_copies[i].wait()
        at = i * (ROWS + OVER)
        ht[:, at : at + ROWS] = hids[i, :, :COL].T
        ht[:, at + ROWS : at + ROWS + OVER] = unfold(hids[i, :, COL:]).T
    outs = []
    for j in range(NG):
        for copy in copies[j]:
            copy.wait()
        rows = []
        for i in range(2):
            rows.append(msgs[i, :, main_cols(j)])
            rows.append(unfold(msgs[i, :, fold_cols(j)]))
        cols = columns(j)
        out[:, cols] = dot(ht[...], jnp.concatenate(rows, axis=0)).astype(BF)
        copy = pltpu.make_async_copy(out.at[:, cols], out_ref.at[:, cols], osem.at[j])
        copy.start()
        outs.append(copy)
    for copy in outs:
        copy.wait()


def weight_rows(dp, own, got):
    return pl.pallas_call(
        grad_kernel,
        in_specs=[IN_SMEM, IN_HBM, IN_HBM],
        out_specs=IN_HBM,
        out_shape=jax.ShapeDtypeStruct((COL, D), BF),
        scratch_shapes=[
            pltpu.VMEM((2, ROWS, NG * BLK), BF),
            pltpu.VMEM((2, ROWS, BLK), BF),
            pltpu.VMEM((COL, 2 * (ROWS + OVER)), BF),
            pltpu.VMEM((COL, D), BF),
            pltpu.SemaphoreType.DMA((NG + 1, 2)),
            pltpu.SemaphoreType.DMA((NG,)),
        ],
        compiler_params=pltpu.CompilerParams(vmem_limit_bytes=44 * 1024 * 1024),
        name="weight_grad",
    )(dp, own, got)


def prepare_kernel(ids_ref, gates_ref, hid_ref, sel_ref, rows_ref, gate_ref):
    r0, r1 = rank_maps(ids_ref[...])
    rows, rank = slots()
    chosen = (dot(rows, assignments(r0, r1)) == rank).astype(F32)
    sel_ref[...] = chosen.T.astype(BF)
    rows_ref[...] = hid_ref[...].reshape(A, F)
    gates = gates_ref[...].astype(F32)
    row, token = iota((A, T), 0), iota((A, T), 1)
    spread = jnp.where(row == 2 * token, gates[0:1, :], 0.0)
    spread += jnp.where(row == 2 * token + 1, gates[1:2, :], 0.0)
    gate = jnp.sum(spread, axis=1, keepdims=True)
    gate_ref[...] = jnp.broadcast_to(gate, (A, 128))


def prepare(ids, gates, hid):
    return pl.pallas_call(
        prepare_kernel,
        in_specs=[IN_VMEM, IN_VMEM, IN_VMEM],
        out_specs=(IN_VMEM, IN_VMEM, IN_VMEM),
        out_shape=(
            pltpu.VMEM((A, ROWS + OVER), BF),
            pltpu.VMEM((A, F), BF),
            pltpu.VMEM((A, 128), F32),
        ),
        compiler_params=PARAMS,
        name="prepare",
    )(ids, gates, hid)


def combine_kernel(sel_ref, ret_ref, gate_ref, hid_ref, out_ref, gg_ref, part):
    over = unfold(ret_ref[:, F:])
    gate = jnp.concatenate([gate_ref[...]] * (COL // 128), axis=1)
    total = None
    for j in range(NH):
        cols = columns(j)
        raw = dot(sel_ref[...], jnp.concatenate([ret_ref[:, cols], over[:, cols]], axis=0))
        out_ref[:, :, cols] = (gate * raw).astype(BF).reshape(T, 2, COL)
        product = hid_ref[:, cols].astype(F32) * raw
        for c in range(COL // 128):
            piece = product[:, columns(c, 128)]
            total = piece if total is None else total + piece
    part[...] = total
    for k in range(2):
        rows = part[pl.ds(k, T, stride=2), :]
        gg_ref[k : k + 1, :] = jnp.sum(rows.T, axis=0, keepdims=True)


def combine(sel, ret, gate, hid):
    return pl.pallas_call(
        combine_kernel,
        in_specs=[IN_VMEM, IN_VMEM, IN_VMEM, IN_VMEM],
        out_specs=(IN_VMEM, IN_VMEM),
        out_shape=(jax.ShapeDtypeStruct((T, 2, F), BF), jax.ShapeDtypeStruct((2, T), F32)),
        scratch_shapes=[pltpu.VMEM((A, 128), F32)],
        compiler_params=PARAMS,
        name="combine",
    )(keep(sel), keep(ret), keep(gate), keep(hid))


def exchange(x):
    width = x.shape[1]
    swapped = lax.all_to_all(
        x.reshape(E, 8, width),
        "expert",
        split_axis=0,
        concat_axis=0,
        axis_index_groups=[[i * 29 % E for i in range(E)]],
        tiled=True,
    )
    return swapped.reshape(ROWS, width)


def swap(x):
    return lax.ppermute(x, "dp", [(0, 1), (1, 0)])


def per_device(hidden, grad_out, gates, expert_ids, weight):
    dp = lax.axis_index("dp").astype(jnp.int32).reshape(1)
    ids = expert_ids.T
    own = weight[0]
    packed = pack(ids, gates.T, grad_out, hidden)
    other = swap(own)
    packed, other, dp = lax.optimization_barrier((packed, other, dp))
    msg = exchange(packed)
    raw, msg = raw_rows(dp, msg, own, other)
    got = swap(msg)
    ids, raw = lax.optimization_barrier((ids, raw))
    ret = exchange(raw)
    sel, hid_rows, gate = prepare(ids, gates.T, hidden)
    weight_grad = weight_rows(dp, msg, got)
    ret, weight_grad = lax.optimization_barrier((ret, weight_grad))
    grad_hidden, grad_gates = combine(sel, ret, gate, hid_rows)
    return grad_hidden, grad_gates.T, weight_grad[None]


def solution(mesh):
    in_specs = (
        P(("dp", "expert"), None, None),
        P(("dp", "expert"), None),
        P(("dp", "expert"), None),
        P(("dp", "expert"), None),
        P("expert", "dp", None),
    )
    out_specs = (
        P(("dp", "expert"), None, None),
        P(("dp", "expert"), None),
        P("expert", "dp", None),
    )
    return jax.shard_map(
        per_device, mesh=mesh, in_specs=in_specs, out_specs=out_specs, check_vma=False
    )
```
